128 devices in a mesh: clip: 4 (over x_hi, core), ctx: 32 (over y, z, x_lo).
Axes of the slice: x: 4 (x_hi: 2, x_lo: 2; x = x_hi * 2 + x_lo), y: 4, z: 4, core: 2. Of those that a mesh axis runs over, the one named last changes fastest.
Arguments:
- queries: bfloat16 [32768, 4096], P(('clip', 'ctx')), parts along dimension 0, may hold values from -128 to 128
- keys: bfloat16 [32768, 4096], P(('clip', 'ctx')), parts along dimension 0, may hold values from -8 to 8
- values: bfloat16 [32768, 4096], P(('clip', 'ctx')), parts along dimension 0, may hold values from -6 to 6
- features: bfloat16 [256, 128, 384], P(('clip', 'ctx')), parts along dimension 0, may hold values from -6 to 6
- feat_grad: bfloat16 [256, 128, 384], P(('clip', 'ctx')), parts along dimension 0, may hold values from -6 to 6
- conv_weight: bfloat16 [3, 384, 384], replicated, may hold values from -0.1875 to 0.1875
- head_weight: bfloat16 [4096, 384], replicated, may hold values from -0.3125 to 0.3125
- pattern: int32 [256, 8], P('clip'), parts along dimension 0, may hold values from 0 to 63, as said below
- live_blocks: int32 [256], P('clip'), parts along dimension 0, may hold values from 1 to 8, as said below
Outputs:
- grad_queries: bfloat16 [32768, 4096], P(('clip', 'ctx')), parts along dimension 0
- grad_keys: bfloat16 [32768, 4096], P(('clip', 'ctx')), parts along dimension 0
- grad_values: bfloat16 [32768, 4096], P(('clip', 'ctx')), parts along dimension 0
- conv_weight_grad: float32 [12, 384, 384], P('clip'), parts along dimension 0
The draws below stay inside these ranges and needn't reach their ends.
There are 4 independent parts, one for each index of `clip`. The reference program is written for one: setup_inputs(seed, part) draws one part's arguments, and reference() takes and returns one part's arrays. A program takes and returns all parts, laid end to end along the dimension named above; an argument that names none is the same for every part. Nothing has to cross between parts.
Inputs may be any that keep to these rules, and one draw needn't show every extreme that they name: `pattern`: row i lists 8 different blocks; its first entry is block i, and the blocks at tile distance 1 to 3 either way, counted cyclically modulo 64, come before others. `live_blocks`: tile 0 has all 8 blocks live.
All inputs are finite; a program needn't handle non-finite values.
Results may differ from the reference program's by a relative error of at most 0.03.
Values may be sent and summed in bfloat16 or wider, within the bound.
No kernel may reach another device: no remote copies, remote signals or barrier semaphores. Data moves between devices by JAX's collectives and lax.ppermute only.
A program may use at most 128 MiB of HBM per device.

```python
import math
import jax
import jax.numpy as jnp
from jax import lax

DH = 128
CV = 384
BLK = 128
NB = 8
PIX = 128
HD = 4096
TOKENS = 8192
FRAMES = 64
NQT = 64


def paired_fields(key):
    first = jax.random.normal(jax.random.fold_in(key, 101), (TOKENS, HD), jnp.float32)
    second = jax.random.normal(jax.random.fold_in(key, 102), (TOKENS, HD), jnp.float32)
    return (jnp.clip(first, -5.0, 5.0), jnp.clip(second, -5.0, 5.0))


def draw_queries(key, part):
    first, second = paired_fields(key)
    return first.astype(jnp.bfloat16)


def draw_keys(key, part):
    first, second = paired_fields(key)
    return second.astype(jnp.bfloat16)


def draw_pattern(key, part):
    key = jax.random.fold_in(key, 5)
    raw = jax.random.randint(key, (NQT, NQT - 1), 0, 1 << 20)
    offsets = jnp.arange(1, NQT, dtype=jnp.int32)
    nearby = (offsets <= 3) | (offsets >= NQT - 3)
    ranked = (raw + jnp.where(nearby, 1 << 21, 0)[None, :]) * NQT + offsets[None, :]
    ignored, picked = lax.top_k(ranked, NB - 1)
    chosen = offsets[picked]
    own = jnp.arange(NQT, dtype=jnp.int32)[:, None]
    others = (own + chosen) % NQT
    return jnp.concatenate([own, others], 1).astype(jnp.int32)


def draw_live_blocks(key, part):
    key = jax.random.fold_in(key, 9)
    counts = jax.random.randint(key, (NQT,), 1, NB + 1)
    return counts.at[0].set(NB).astype(jnp.int32)


def shard_levels(own_key, shape, shards, least, top_value):
    loudness = 1.0
    for dim, parts in shards:
        heights = jax.random.uniform(jax.random.fold_in(jax.random.fold_in(own_key, 6), dim), (parts,), jnp.float32, least / len(shards), top_value / len(shards))
        loudness = loudness * jnp.repeat(jnp.exp(heights), shape[dim] // parts).reshape((-1,) + (1,) * (len(shape) - 1 - dim))
    return loudness


def noise(key, extent, scale, bound, split=(), kind=jnp.bfloat16):
    result = scale * jax.random.normal(key, extent, jnp.float32)
    if split:
        result = result * shard_levels(key, extent, split, -0.22, 0.18)
    return jnp.clip(result, -bound, bound).astype(kind)


def setup_inputs(seed: int = 0, part: int = 0) -> dict:
    key_of = jax.random.split(jax.random.key(seed), 10)
    part_splits = jax.random.split(jax.random.fold_in(key_of[9], part), 10)
    queries = draw_queries(jax.random.fold_in(jax.random.fold_in(key_of[9], part), 71), part)
    keys = draw_keys(jax.random.fold_in(jax.random.fold_in(key_of[9], part), 71), part)
    values = noise(part_splits[2], (TOKENS, HD), 1.0, 6.0, ((0, 32),))
    features = noise(part_splits[3], (FRAMES, PIX, CV), 1.0, 6.0, ((0, 32),))
    feat_grad = noise(part_splits[4], (FRAMES, PIX, CV), 1.0, 6.0, ((0, 32),))
    conv_weight = noise(key_of[5], (3, CV, CV), (3 * CV) ** -0.5, 0.1875)
    head_weight = noise(key_of[6], (HD, CV), CV ** -0.5, 0.3125)
    pattern = draw_pattern(jax.random.fold_in(jax.random.fold_in(key_of[9], part), 71), part)
    live_blocks = draw_live_blocks(jax.random.fold_in(jax.random.fold_in(key_of[9], part), 71), part)
    return {"queries": queries, "keys": keys, "values": values, "features": features, "feat_grad": feat_grad, "conv_weight": conv_weight, "head_weight": head_weight, "pattern": pattern, "live_blocks": live_blocks}


def sparse_attention_grads(queries, keys, values, attn_grad, pattern, live_blocks):
    total = queries.shape[0]
    heads = queries.shape[1] // DH
    tiles = total // BLK
    scale = DH ** (-0.5)
    query_all = queries.reshape(tiles, BLK, heads, DH)
    key_all = keys.reshape(tiles, BLK, heads, DH)
    value_all = values.reshape(tiles, BLK, heads, DH)
    grad_all = attn_grad.reshape(tiles, BLK, heads, DH)
    listed = pattern.shape[1]

    def group_step(carry, group):
        key_acc, value_acc = carry
        start = (group * 4).astype(jnp.int32)
        rows = lax.dynamic_slice_in_dim(pattern, start, 4, 0)
        counts = lax.dynamic_slice_in_dim(live_blocks, start, 4, 0)
        query_tile = lax.dynamic_slice_in_dim(query_all, start, 4, 0).astype(jnp.float32)
        grad_tile = lax.dynamic_slice_in_dim(grad_all, start, 4, 0).astype(jnp.float32)
        key_rows = key_all[rows].astype(jnp.float32)
        value_rows = value_all[rows].astype(jnp.float32)
        scores = jnp.einsum('gqhd,gnkhd->ghqnk', query_tile, key_rows) * scale
        usable = jnp.arange(listed, dtype=jnp.int32)[None, :] < counts[:, None]
        scores = jnp.where(usable[:, None, None, :, None], scores, -jnp.inf)
        top = lax.optimization_barrier(jnp.max(scores, axis=(3, 4), keepdims=True))
        weights = jnp.exp(scores - top)
        probs = weights / lax.optimization_barrier(jnp.sum(weights, axis=(3, 4), keepdims=True))
        probs_bf = lax.optimization_barrier(probs.astype(jnp.bfloat16)).astype(jnp.float32)
        attn_out = jnp.einsum('ghqnk,gnkhd->gqhd', probs_bf, value_rows)
        delta = jnp.einsum('gqhd,gqhd->ghq', grad_tile, attn_out)
        dprobs = jnp.einsum('gqhd,gnkhd->ghqnk', grad_tile, value_rows)
        dscores = probs * (dprobs - delta[:, :, :, None, None])
        dscores_bf = lax.optimization_barrier(dscores.astype(jnp.bfloat16)).astype(jnp.float32)
        grad_query = jnp.einsum('ghqnk,gnkhd->gqhd', dscores_bf, key_rows) * scale
        key_part = jnp.einsum('ghqnk,gqhd->gnkhd', dscores_bf, query_tile) * scale
        value_part = jnp.einsum('ghqnk,gqhd->gnkhd', probs_bf, grad_tile)
        key_acc = key_acc.at[rows].add(key_part)
        value_acc = value_acc.at[rows].add(value_part)
        return ((key_acc, value_acc), grad_query.astype(jnp.bfloat16))
    empty = jnp.zeros((tiles, BLK, heads, DH), jnp.float32)
    (key_acc, value_acc), grad_query = lax.scan(group_step, (empty, empty), jnp.arange(tiles // 4, dtype=jnp.int32))
    width = heads * DH
    return (grad_query.reshape(total, width), key_acc.reshape(total, width).astype(jnp.bfloat16), value_acc.reshape(total, width).astype(jnp.bfloat16))

def reference(queries, keys, values, features, feat_grad, conv_weight, head_weight, pattern, live_blocks):
    frames = features.shape[0]
    channels = features.shape[2]
    padded = jnp.concatenate([feat_grad, jnp.zeros((2,) + feat_grad.shape[1:], feat_grad.dtype)], 0)
    flat_features = features.reshape(-1, channels)
    summed = jnp.zeros((flat_features.shape[0], channels), jnp.float32)
    tap_grads = []
    for kernel_tap in range(3):
        window = padded[kernel_tap:kernel_tap + frames].reshape(-1, channels)
        summed = summed + jnp.dot(window, conv_weight[kernel_tap].T, preferred_element_type=jnp.float32)
        tap_grads.append(jnp.dot(flat_features.T, window, preferred_element_type=jnp.float32))
    feature_grad = summed.astype(jnp.bfloat16)
    conv_weight_grad = jnp.stack(tap_grads, 0) * (1.0 / math.sqrt(TOKENS))
    attn_grad = jnp.dot(feature_grad, head_weight.T, preferred_element_type=jnp.float32).astype(jnp.bfloat16)
    grad_queries, grad_keys, grad_values = sparse_attention_grads(queries, keys, values, attn_grad, pattern, live_blocks)
    return (grad_queries, grad_keys, grad_values, conv_weight_grad)
```

```python
import functools
import math

import jax
import jax.numpy as jnp
from jax import lax
from jax.experimental import pallas as pl
from jax.experimental.pallas import tpu as pltpu
from jax.sharding import PartitionSpec as P

DH = 128
BLK = 128
GROUP = 8
NT = (((1,), (1,)), ((), ()))
TN = (((0,), (0,)), ((), ()))
F32 = jnp.float32
BF16 = jnp.bfloat16
VMEM_LIMIT = 60 * 1024 * 1024


def first_row(tile, stride):
    return pl.multiple_of((tile >> 1) * stride + (tile & 1) * BLK, BLK)


def by_count(count, most, body):
    for size in range(1, most + 1):
        pl.when(count == size)(functools.partial(body, size))


def pack_pair_kernel(first_ref, second_ref, out_ref):
    rows = first_ref.shape[0]
    for head in range(out_ref.shape[0]):
        columns = slice(head * DH, (head + 1) * DH)
        out_ref[head, :rows, :] = first_ref[:, columns]
        out_ref[head, rows:, :] = second_ref[:, columns]


def pack_pair(first, second):
    rows, width = first.shape
    heads = width // DH
    group = 4
    return pl.pallas_call(
        pack_pair_kernel,
        grid=(heads // group,),
        in_specs=[pl.BlockSpec((rows, group * DH), lambda i: (0, i))] * 2,
        out_specs=pl.BlockSpec((group, 2 * rows, DH), lambda i: (i, 0, 0)),
        out_shape=jax.ShapeDtypeStruct((heads, 2 * rows, DH), first.dtype),
        compiler_params=pltpu.CompilerParams(vmem_limit_bytes=VMEM_LIMIT),
        cost_estimate=pl.CostEstimate(flops=0, bytes_accessed=8 * rows * width, transcendentals=0),
    )(first, second)


def pack_project_kernel(value_ref, grad_ref, weight_ref, out_ref):
    rows = value_ref.shape[0]
    projected = lax.dot_general(
        grad_ref[...], weight_ref[...], NT, preferred_element_type=F32
    ).astype(BF16)
    for head in range(out_ref.shape[0]):
        columns = slice(head * DH, (head + 1) * DH)
        out_ref[head, :rows, :] = value_ref[:, columns]
        out_ref[head, rows:, :] = projected[:, columns]


def pack_project(values, feature_grad, head_weight):
    rows, width = values.shape
    heads = width // DH
    channels = feature_grad.shape[1]
    group = 4
    return pl.pallas_call(
        pack_project_kernel,
        grid=(heads // group,),
        in_specs=[
            pl.BlockSpec((rows, group * DH), lambda i: (0, i)),
            pl.BlockSpec((rows, channels), lambda i: (0, 0)),
            pl.BlockSpec((group * DH, channels), lambda i: (i, 0)),
        ],
        out_specs=pl.BlockSpec((group, 2 * rows, DH), lambda i: (i, 0, 0)),
        out_shape=jax.ShapeDtypeStruct((heads, 2 * rows, DH), values.dtype),
        compiler_params=pltpu.CompilerParams(vmem_limit_bytes=VMEM_LIMIT),
        cost_estimate=pl.CostEstimate(
            flops=2 * rows * width * channels, bytes_accessed=8 * rows * width, transcendentals=0
        ),
    )(values, feature_grad, head_weight)


def unpack_kernel(packed_ref, *out_refs):
    rows = out_refs[0].shape[0]
    for head in range(packed_ref.shape[0]):
        for place, out_ref in enumerate(out_refs):
            out_ref[:, head * DH : (head + 1) * DH] = packed_ref[
                head, place * rows : (place + 1) * rows, :
            ]


def unpack(packed, count):
    heads, total, _ = packed.shape
    rows = total // count
    group = 4
    return pl.pallas_call(
        unpack_kernel,
        grid=(heads // group,),
        in_specs=[pl.BlockSpec((group, total, DH), lambda i: (i, 0, 0))],
        out_specs=[pl.BlockSpec((rows, group * DH), lambda i: (0, i))] * count,
        out_shape=[jax.ShapeDtypeStruct((rows, heads * DH), packed.dtype)] * count,
        compiler_params=pltpu.CompilerParams(vmem_limit_bytes=VMEM_LIMIT),
        cost_estimate=pl.CostEstimate(
            flops=0, bytes_accessed=4 * heads * total * DH, transcendentals=0
        ),
    )(packed)


def probs_kernel(listed, pattern, live, qk_ref, probs_ref, key_t_ref):
    stride = 4 * BLK
    scale = DH ** (-0.5) * math.log2(math.e)

    def tile_step(place, carry):
        tile = pl.program_id(0) * GROUP + place
        own = first_row(tile, stride)
        query = qk_ref[pl.ds(own, BLK), :]
        key_t_ref[place] = qk_ref[pl.ds(own + 2 * BLK, BLK), :].T

        def body(size):
            blocks = [pattern[tile * listed + j] for j in range(size)]
            keys = jnp.concatenate(
                [qk_ref[pl.ds(first_row(b, stride) + 2 * BLK, BLK), :] for b in blocks], 0
            )
            scores = lax.dot_general(keys, query, NT, preferred_element_type=F32)
            top = jnp.max(scores, axis=0, keepdims=True)
            weights = jnp.exp2((scores - top) * scale)
            inverse = 1.0 / jnp.sum(weights, axis=0, keepdims=True)
            probs_ref[place, : size * BLK, :] = (weights * inverse).astype(BF16)

        by_count(live[tile], listed, body)
        return carry

    lax.fori_loop(0, GROUP, tile_step, 0)


def probs_of(qk, pattern, live_blocks):
    tiles, listed = pattern.shape
    pairs = tiles * listed
    return pl.pallas_call(
        functools.partial(probs_kernel, listed),
        grid_spec=pltpu.PrefetchScalarGridSpec(
            num_scalar_prefetch=2,
            grid=(tiles // GROUP,),
            in_specs=[pl.BlockSpec(qk.shape, lambda i, *_: (0, 0))],
            out_specs=[
                pl.BlockSpec((GROUP, listed * BLK, BLK), lambda i, *_: (i, 0, 0)),
                pl.BlockSpec((GROUP, DH, BLK), lambda i, *_: (i, 0, 0)),
            ],
        ),
        out_shape=[
            jax.ShapeDtypeStruct((tiles, listed * BLK, BLK), BF16),
            jax.ShapeDtypeStruct((tiles, DH, BLK), BF16),
        ],
        compiler_params=pltpu.CompilerParams(vmem_limit_bytes=VMEM_LIMIT),
        cost_estimate=pl.CostEstimate(
            flops=2 * pairs * BLK * BLK * DH,
            bytes_accessed=2 * pairs * BLK * BLK,
            transcendentals=pairs * BLK * BLK,
        ),
    )(pattern.reshape(-1), live_blocks, qk)


def grads_kernel(
    listed, tiles, pattern, live, qk_ref, vg_ref, key_t_ref, probs_ref, out_ref, total_ref
):
    stride = 4 * BLK
    out_stride = 6 * BLK
    scale = DH ** (-0.5)

    @pl.when(pl.program_id(0) == 0)
    def _():
        def clear(block, carry):
            total_ref[block] = jnp.zeros(total_ref.shape[1:], F32)
            return carry

        lax.fori_loop(0, tiles, clear, 0)

    def tile_step(place, carry):
        tile = pl.program_id(0) * GROUP + place
        own = first_row(tile, stride)
        query = qk_ref[pl.ds(own, BLK), :]
        grad = vg_ref[pl.ds(own + 2 * BLK, BLK), :]
        empty = jnp.zeros_like(query)
        both = jnp.concatenate(
            [jnp.concatenate([grad, empty], 1), jnp.concatenate([empty, query], 1)], 0
        )

        def body(size):
            blocks = [pattern[tile * listed + j] for j in range(size)]
            values = jnp.concatenate([vg_ref[pl.ds(first_row(b, stride), BLK), :] for b in blocks], 0)
            dprobs = lax.dot_general(values, grad, NT, preferred_element_type=F32)
            probs_bf = probs_ref[place, : size * BLK, :]
            probs = probs_bf.astype(F32)
            delta = jnp.sum(probs * dprobs, axis=0, keepdims=True)
            dscores = (probs * (dprobs - delta)).astype(BF16)
            terms = jnp.dot(
                jnp.concatenate([probs_bf, dscores], 1), both, preferred_element_type=F32
            )
            for j, b in enumerate(blocks):
                total_ref[b] += terms[j * BLK : (j + 1) * BLK, :]
            keys_t = jnp.concatenate([key_t_ref[b] for b in blocks], 1)
            query_grad = jnp.dot(keys_t, dscores, preferred_element_type=F32)
            out_ref[pl.ds(first_row(tile, out_stride), BLK), :] = (query_grad * scale).T.astype(BF16)

        by_count(live[tile], listed, body)
        return carry

    lax.fori_loop(0, GROUP, tile_step, 0)

    @pl.when(pl.program_id(0) == pl.num_programs(0) - 1)
    def _():
        def finish(block, carry):
            row = first_row(block, out_stride)
            total = total_ref[block]
            out_ref[pl.ds(row + 2 * BLK, BLK), :] = (total[:, DH:] * scale).astype(BF16)
            out_ref[pl.ds(row + 4 * BLK, BLK), :] = total[:, :DH].astype(BF16)
            return carry

        lax.fori_loop(0, tiles, finish, 0)


def grads_of(qk, vg, keys_t, probs, pattern, live_blocks):
    tiles, listed = pattern.shape
    pairs = tiles * listed
    rows = 3 * tiles * BLK
    return pl.pallas_call(
        functools.partial(grads_kernel, listed, tiles),
        grid_spec=pltpu.PrefetchScalarGridSpec(
            num_scalar_prefetch=2,
            grid=(tiles // GROUP,),
            in_specs=[
                pl.BlockSpec(qk.shape, lambda i, *_: (0, 0)),
                pl.BlockSpec(vg.shape, lambda i, *_: (0, 0)),
                pl.BlockSpec(keys_t.shape, lambda i, *_: (0, 0, 0)),
                pl.BlockSpec((GROUP, listed * BLK, BLK), lambda i, *_: (i, 0, 0)),
            ],
            out_specs=pl.BlockSpec((rows, DH), lambda i, *_: (0, 0)),
            scratch_shapes=[pltpu.VMEM((tiles, BLK, 2 * DH), F32)],
        ),
        out_shape=jax.ShapeDtypeStruct((rows, DH), BF16),
        compiler_params=pltpu.CompilerParams(vmem_limit_bytes=VMEM_LIMIT),
        cost_estimate=pl.CostEstimate(
            flops=8 * pairs * BLK * BLK * DH,
            bytes_accessed=2 * pairs * BLK * BLK + 16 * tiles * BLK * DH,
            transcendentals=0,
        ),
    )(pattern.reshape(-1), live_blocks, qk, vg, keys_t, probs)


def exchange(blocks):
    return lax.all_to_all(blocks, "ctx", split_axis=0, concat_axis=0, tiled=True)


def body(
    queries, keys, values, features, feat_grad, conv_weight, head_weight, pattern, live_blocks
):
    devices = lax.axis_size("ctx")
    frames, positions, channels = features.shape
    taps = conv_weight.shape[0]
    rows = frames * positions

    qk = exchange(pack_pair(queries, keys)).reshape(-1, DH)

    incoming = lax.ppermute(feat_grad, "ctx", [(i + 1, i) for i in range(devices - 1)])
    extended = jnp.concatenate([feat_grad, incoming], 0)
    windows = [extended[k : k + frames].reshape(rows, channels) for k in range(taps)]
    summed = sum(
        lax.dot_general(windows[k], conv_weight[k], NT, preferred_element_type=F32)
        for k in range(taps)
    )
    flat_features = features.reshape(rows, channels)
    tap_terms = jnp.stack(
        [
            lax.dot_general(flat_features, windows[k], TN, preferred_element_type=F32)
            for k in range(taps)
        ],
        0,
    ).astype(BF16)
    vg = exchange(pack_project(values, summed.astype(BF16), head_weight)).reshape(-1, DH)

    probs, keys_t = probs_of(qk, pattern, live_blocks)

    tap_terms, vg = lax.optimization_barrier((tap_terms, vg))
    share = taps * channels // devices
    tap_terms = exchange(tap_terms.reshape(devices, share, channels))
    tap_share = jnp.sum(tap_terms.astype(F32), axis=0).astype(BF16)

    grads = grads_of(qk, vg, keys_t, probs, pattern, live_blocks)
    grads, tap_share = lax.optimization_barrier((grads, tap_share))
    tap_total = lax.all_gather(tap_share, "ctx").reshape(conv_weight.shape).astype(F32)
    token_count = rows * devices
    conv_weight_grad = tap_total * (1.0 / math.sqrt(token_count))

    received = exchange(grads.reshape(devices, 3 * rows, DH))
    grad_queries, grad_keys, grad_values = unpack(received, 3)
    return (grad_queries, grad_keys, grad_values, conv_weight_grad)


def solution(mesh):
    placed = (
        P(("clip", "ctx"), None),
        P(("clip", "ctx"), None),
        P(("clip", "ctx"), None),
        P(("clip", "ctx"), None, None),
        P(("clip", "ctx"), None, None),
        P(),
        P(),
        P("clip", None),
        P("clip"),
    )
    return jax.shard_map(
        body,
        mesh=mesh,
        in_specs=placed,
        out_specs=(
            P(("clip", "ctx"), None),
            P(("clip", "ctx"), None),
            P(("clip", "ctx"), None),
            P("clip", None, None),
        ),
        check_vma=False,
    )
```

```python
import functools
import math

import jax
import jax.numpy as jnp
from jax import lax
from jax.experimental import pallas as pl
from jax.experimental.pallas import tpu as pltpu
from jax.sharding import PartitionSpec as P

DH = 128
BLK = 128
TOGETHER = 4
GROUP = 8
NT = (((1,), (1,)), ((), ()))
TN = (((0,), (0,)), ((), ()))
F32 = jnp.float32
BF16 = jnp.bfloat16
KERNEL_LIMIT = 56 * 1024 * 1024
HBM_SPEC = pl.BlockSpec(memory_space=pl.ANY)
VMEM_SPEC = pl.BlockSpec(memory_space=pltpu.VMEM)


def rows_of(tile):
    return tile >> 1, pl.ds(pl.multiple_of((tile & 1) * BLK, BLK), BLK)


def by_count(count, most, body):
    for size in range(1, most + 1):
        pl.when(count == size)(functools.partial(body, size))


def order_by_count(live_blocks):
    tiles = live_blocks.shape[0]
    ids = jnp.arange(tiles, dtype=jnp.int32)
    here, there = live_blocks[:, None], live_blocks[None, :]
    ahead = (there > here) | ((there == here) & (ids[None, :] < ids[:, None]))
    rank = jnp.sum(ahead.astype(jnp.int32), axis=1)
    placed = (rank[None, :] == ids[:, None]).astype(jnp.int32)
    return jnp.sum(placed * ids[None, :], axis=1)


def columns_of(ref, head):
    return ref.at[:, pl.ds(head * DH, DH)]


def move(copies):
    for copy in copies:
        copy.start()
    for copy in copies:
        copy.wait()


def pack_kernel(first_ref, out_ref, sems):
    move(
        [
            pltpu.make_async_copy(columns_of(first_ref, head), out_ref.at[head], sems.at[head])
            for head in range(out_ref.shape[0])
        ]
    )


def pack(array):
    rows, width = array.shape
    heads = width // DH
    return pl.pallas_call(
        pack_kernel,
        in_specs=[HBM_SPEC],
        out_specs=HBM_SPEC,
        out_shape=jax.ShapeDtypeStruct((heads, rows, DH), array.dtype),
        scratch_shapes=[pltpu.SemaphoreType.DMA((heads,))],
        cost_estimate=pl.CostEstimate(flops=0, bytes_accessed=4 * rows * width, transcendentals=0),
    )(array)


def pack_taps_kernel(first_ref, tap_ref, out_ref, sems):
    heads, rows = out_ref.shape[0], first_ref.shape[0]
    copies = [
        pltpu.make_async_copy(
            columns_of(first_ref, head), out_ref.at[head, pl.ds(0, rows), :], sems.at[head]
        )
        for head in range(heads)
    ]
    copies.append(
        pltpu.make_async_copy(
            tap_ref, out_ref.at[:, pl.ds(rows, tap_ref.shape[1]), :], sems.at[heads]
        )
    )
    move(copies)


def pack_taps(array, taps):
    rows, width = array.shape
    heads = width // DH
    return pl.pallas_call(
        pack_taps_kernel,
        in_specs=[HBM_SPEC, HBM_SPEC],
        out_specs=HBM_SPEC,
        out_shape=jax.ShapeDtypeStruct((heads, rows + taps.shape[1], DH), array.dtype),
        scratch_shapes=[pltpu.SemaphoreType.DMA((heads + 1,))],
        cost_estimate=pl.CostEstimate(flops=0, bytes_accessed=4 * rows * width, transcendentals=0),
    )(array, taps)


def pack_project_kernel(key_ref, grad_ref, weight_ref, out_ref, sems):
    heads, rows = out_ref.shape[0], key_ref.shape[0]
    copies = [
        pltpu.make_async_copy(
            columns_of(key_ref, head), out_ref.at[head, pl.ds(0, rows), :], sems.at[head]
        )
        for head in range(heads)
    ]
    for copy in copies:
        copy.start()
    for head in range(0, heads, 2):
        projected = lax.dot_general(
            grad_ref[...], weight_ref[head * DH : (head + 2) * DH, :], NT, preferred_element_type=F32
        ).astype(BF16)
        out_ref[head, rows:, :] = projected[:, :DH]
        out_ref[head + 1, rows:, :] = projected[:, DH:]
    for copy in copies:
        copy.wait()


def pack_project(keys, feature_grad, head_weight):
    rows, width = keys.shape
    heads = width // DH
    channels = feature_grad.shape[1]
    return pl.pallas_call(
        pack_project_kernel,
        in_specs=[HBM_SPEC, VMEM_SPEC, VMEM_SPEC],
        out_specs=VMEM_SPEC,
        out_shape=jax.ShapeDtypeStruct((heads, 2 * rows, DH), keys.dtype),
        scratch_shapes=[pltpu.SemaphoreType.DMA((heads,))],
        compiler_params=pltpu.CompilerParams(vmem_limit_bytes=KERNEL_LIMIT),
        cost_estimate=pl.CostEstimate(
            flops=2 * rows * width * channels, bytes_accessed=8 * rows * width, transcendentals=0
        ),
    )(keys, feature_grad, head_weight)


def unpack_kernel(pair_ref, last_ref, *refs):
    out_refs, sems = refs[:-1], refs[-1]
    rows = out_refs[0].shape[0]
    sources = [(pair_ref, 0), (pair_ref, rows), (last_ref, 0)]
    move(
        [
            pltpu.make_async_copy(
                ref.at[head, pl.ds(start, rows), :], columns_of(out_ref, head), sems.at[place, head]
            )
            for place, ((ref, start), out_ref) in enumerate(zip(sources, out_refs))
            for head in range(pair_ref.shape[0])
        ]
    )


def unpack(pair, last):
    heads, rows, _ = last.shape
    return pl.pallas_call(
        unpack_kernel,
        in_specs=[HBM_SPEC] * 2,
        out_specs=[HBM_SPEC] * 3,
        out_shape=[jax.ShapeDtypeStruct((rows, heads * DH), last.dtype)] * 3,
        scratch_shapes=[pltpu.SemaphoreType.DMA((3, heads))],
        cost_estimate=pl.CostEstimate(
            flops=0, bytes_accessed=12 * rows * heads * DH, transcendentals=0
        ),
    )(pair, last)


def clear(total_ref):
    def step(block, carry):
        total_ref[block] = jnp.zeros(total_ref.shape[1:], F32)
        return carry

    lax.fori_loop(0, total_ref.shape[0], step, 0)


def gather(ref, blocks, base=0):
    return jnp.concatenate(
        [ref[b >> 1, pl.ds(pl.multiple_of((b & 1) * BLK + base, BLK), BLK), :] for b in blocks], 0
    )


def probs_kernel(
    listed, pattern, live, order, query_ref, key_ref, grad_ref, probs_ref, key_t_ref, out_ref, total_ref
):
    scale = DH ** (-0.5) * math.log2(math.e)
    step, steps = pl.program_id(0), pl.num_programs(0)

    @pl.when(step == 0)
    def _():
        clear(total_ref)

    def group_step(group, carry):
        slots = [group * TOGETHER + t for t in range(TOGETHER)]
        tiles = [order[step * GROUP + slot] for slot in slots]

        def body(size):
            held = []
            for slot, tile in zip(slots, tiles):
                query = query_ref[rows_of(tile)]
                blocks = [pattern[tile * listed + j] for j in range(size)]
                scores = lax.dot_general(
                    gather(key_ref, blocks), query, NT, preferred_element_type=F32
                )
                key_block = lax.broadcasted_iota(jnp.int32, scores.shape, 0) >> 7
                scores = jnp.where(key_block < live[tile], scores, -jnp.inf)
                top = jnp.max(scores, axis=0, keepdims=True)
                weights = jnp.exp2((scores - top) * scale)
                inverse = 1.0 / jnp.sum(weights, axis=0, keepdims=True)
                probs = (weights * inverse).astype(BF16)
                probs_ref[slot, : size * BLK, :] = probs
                terms = jnp.dot(probs, grad_ref[rows_of(tile)], preferred_element_type=F32)
                held.append((blocks, terms))
            for blocks, terms in held:
                for j, b in enumerate(blocks):
                    total_ref[b] += terms[j * BLK : (j + 1) * BLK, :]

        by_count(live[tiles[0]], listed, body)
        for slot in slots:
            key_t_ref[slot] = key_ref[rows_of(step * GROUP + slot)].T
        return carry

    lax.fori_loop(0, GROUP // TOGETHER, group_step, 0)

    @pl.when(step == steps - 1)
    def _():
        def finish(block, carry):
            out_ref[rows_of(block)] = total_ref[block].astype(BF16)
            return carry

        lax.fori_loop(0, total_ref.shape[0], finish, 0)


def whole(shape, index=None):
    index = (0,) * len(shape) if index is None else index
    return pl.BlockSpec(shape, lambda i, *_: index, pipeline_mode=pl.Buffered(1))


def probs_of(query, pair, pattern, live_blocks, order):
    tiles, listed = pattern.shape
    pairs = tiles * listed
    return pl.pallas_call(
        functools.partial(probs_kernel, listed),
        grid_spec=pltpu.PrefetchScalarGridSpec(
            num_scalar_prefetch=3,
            grid=(tiles // GROUP,),
            in_specs=[whole(query.shape), whole(query.shape), whole(query.shape, (0, 1, 0))],
            out_specs=[
                pl.BlockSpec((GROUP, listed * BLK, BLK), lambda i, *_: (i, 0, 0)),
                pl.BlockSpec((GROUP, DH, BLK), lambda i, *_: (i, 0, 0)),
                whole(query.shape),
            ],
            scratch_shapes=[pltpu.VMEM((tiles, BLK, DH), F32)],
        ),
        out_shape=[
            jax.ShapeDtypeStruct((tiles, listed * BLK, BLK), BF16),
            jax.ShapeDtypeStruct((tiles, DH, BLK), BF16),
            jax.ShapeDtypeStruct(query.shape, BF16),
        ],
        compiler_params=pltpu.CompilerParams(vmem_limit_bytes=KERNEL_LIMIT),
        cost_estimate=pl.CostEstimate(
            flops=4 * pairs * BLK * BLK * DH,
            bytes_accessed=2 * pairs * BLK * BLK,
            transcendentals=pairs * BLK * BLK,
        ),
    )(pattern.reshape(-1), live_blocks, order, query, pair, pair)


def grads_kernel(
    listed, pattern, live, order, query_ref, grad_ref, value_ref, key_t_ref, probs_ref, out_ref, total_ref
):
    scale = DH ** (-0.5)
    step, steps = pl.program_id(0), pl.num_programs(0)
    rows = query_ref.shape[1]

    @pl.when(step == 0)
    def _():
        clear(total_ref)
        shares = jnp.sum(value_ref[:, rows:, :].astype(F32), axis=0)
        out_ref[:, 2 * rows :, :] = jnp.broadcast_to(
            shares.astype(BF16)[None], (out_ref.shape[0],) + shares.shape
        )

    def group_step(group, carry):
        slots = [group * TOGETHER + t for t in range(TOGETHER)]
        members = [order[step * GROUP + slot] for slot in slots]

        def body(size):
            held = []
            for slot, tile in zip(slots, members):
                blocks = [pattern[tile * listed + j] for j in range(size)]
                dprobs = lax.dot_general(
                    gather(value_ref, blocks), grad_ref[rows_of(tile)], NT, preferred_element_type=F32
                )
                probs = probs_ref[slot, : size * BLK, :].astype(F32)
                delta = jnp.sum(probs * dprobs, axis=0, keepdims=True)
                dscores = (probs * (dprobs - delta)).astype(BF16)
                keys_t = jnp.concatenate([key_t_ref[b] for b in blocks], 1)
                query_grad = jnp.dot(keys_t, dscores, preferred_element_type=F32)
                out_ref[rows_of(tile)] = (query_grad * scale).T.astype(BF16)
                terms = jnp.dot(dscores, query_ref[rows_of(tile)], preferred_element_type=F32)
                held.append((blocks, terms))
            for blocks, terms in held:
                for j, b in enumerate(blocks):
                    total_ref[b] += terms[j * BLK : (j + 1) * BLK, :]

        by_count(live[members[0]], listed, body)
        return carry

    lax.fori_loop(0, GROUP // TOGETHER, group_step, 0)

    @pl.when(step == steps - 1)
    def _():
        def finish(block, carry):
            start = pl.multiple_of((block & 1) * BLK + rows, BLK)
            out_ref[block >> 1, pl.ds(start, BLK), :] = (total_ref[block] * scale).astype(BF16)
            return carry

        lax.fori_loop(0, total_ref.shape[0], finish, 0)


def grads_of(query, pair, value_taps, keys_t, probs, pattern, live_blocks, order):
    tiles, listed = pattern.shape
    pairs = tiles * listed
    devices, rows, _ = query.shape
    held = rows + value_taps.shape[1]
    return pl.pallas_call(
        functools.partial(grads_kernel, listed),
        grid_spec=pltpu.PrefetchScalarGridSpec(
            num_scalar_prefetch=3,
            grid=(tiles // GROUP,),
            in_specs=[
                whole(query.shape),
                whole(query.shape, (0, 1, 0)),
                whole(value_taps.shape),
                whole(keys_t.shape),
                pl.BlockSpec((GROUP, listed * BLK, BLK), lambda i, *_: (i, 0, 0)),
            ],
            out_specs=whole((devices, held, DH)),
            scratch_shapes=[pltpu.VMEM((tiles, BLK, DH), F32)],
        ),
        out_shape=jax.ShapeDtypeStruct((devices, held, DH), BF16),
        compiler_params=pltpu.CompilerParams(vmem_limit_bytes=KERNEL_LIMIT),
        cost_estimate=pl.CostEstimate(
            flops=6 * pairs * BLK * BLK * DH,
            bytes_accessed=2 * pairs * BLK * BLK + 16 * tiles * BLK * DH,
            transcendentals=0,
        ),
    )(pattern.reshape(-1), live_blocks, order, query, pair, value_taps, keys_t, probs)


def exchange(blocks):
    return lax.all_to_all(blocks, "ctx", split_axis=0, concat_axis=0, tiled=True)


def body(
    queries, keys, values, features, feat_grad, conv_weight, head_weight, pattern, live_blocks
):
    devices = lax.axis_size("ctx")
    frames, positions, channels = features.shape
    taps = conv_weight.shape[0]
    rows = frames * positions

    incoming = lax.ppermute(feat_grad, "ctx", [(i + 1, i) for i in range(devices - 1)])
    packed = pack(queries)
    packed, incoming, feat_grad = lax.optimization_barrier((packed, incoming, feat_grad))
    query = exchange(packed)

    order = order_by_count(live_blocks)
    extended = jnp.concatenate([feat_grad, incoming], 0)
    windows = [extended[k : k + frames].reshape(rows, channels) for k in range(taps)]
    summed = sum(
        lax.dot_general(windows[k], conv_weight[k], NT, preferred_element_type=F32)
        for k in range(taps)
    )
    flat_features = features.reshape(rows, channels)
    tap_terms = jnp.stack(
        [
            lax.dot_general(flat_features, windows[k], TN, preferred_element_type=F32)
            for k in range(taps)
        ],
        0,
    ).astype(BF16)
    share = tap_terms.size // devices // DH
    held = -(-share // 16) * 16
    tap_terms = jnp.pad(tap_terms.reshape(devices, share, DH), ((0, 0), (0, held - share), (0, 0)))
    pair = pack_project(keys, summed.astype(BF16), head_weight)
    value_taps = pack_taps(values, tap_terms)
    pair, value_taps, query, order = lax.optimization_barrier((pair, value_taps, query, order))

    pair = exchange(pair)
    value_taps, pair = lax.optimization_barrier((value_taps, pair))
    value_taps = exchange(value_taps)
    probs, keys_t, value_grad = probs_of(query, pair, pattern, live_blocks, order)

    value_taps, value_grad = lax.optimization_barrier((value_taps, value_grad))
    value_grad = exchange(value_grad)
    grads = grads_of(query, pair, value_taps, keys_t, probs, pattern, live_blocks, order)
    grads, value_grad = lax.optimization_barrier((grads, value_grad))
    grads = exchange(grads)

    grad_queries, grad_keys, grad_values = unpack(grads, value_grad)
    tap_total = grads[:, 2 * rows : 2 * rows + share, :].reshape(conv_weight.shape).astype(F32)
    token_count = rows * devices
    conv_weight_grad = tap_total * (1.0 / math.sqrt(token_count))
    return (grad_queries, grad_keys, grad_values, conv_weight_grad)


def solution(mesh):
    placed = (
        P(("clip", "ctx"), None),
        P(("clip", "ctx"), None),
        P(("clip", "ctx"), None),
        P(("clip", "ctx"), None, None),
        P(("clip", "ctx"), None, None),
        P(),
        P(),
        P("clip", None),
        P("clip"),
    )
    return jax.shard_map(
        body,
        mesh=mesh,
        in_specs=placed,
        out_specs=(
            P(("clip", "ctx"), None),
            P(("clip", "ctx"), None),
            P(("clip", "ctx"), None),
            P("clip", None, None),
        ),
        check_vma=False,
    )
```

```python
import functools
import math

import jax
import jax.numpy as jnp
from jax import lax
from jax.experimental import pallas as pl
from jax.experimental.pallas import tpu as pltpu
from jax.sharding import PartitionSpec as P

DH = 128
BLK = 128
TOGETHER = 4
GROUP = 8
PACKED = 4
NT = (((1,), (1,)), ((), ()))
TN = (((0,), (0,)), ((), ()))
F32 = jnp.float32
BF16 = jnp.bfloat16
KERNEL_LIMIT = 56 * 1024 * 1024
SMALL_LIMIT = 16 * 1024 * 1024
HBM_SPEC = pl.BlockSpec(memory_space=pl.ANY)
VMEM_SPEC = pl.BlockSpec(memory_space=pltpu.VMEM)


def rows_of(tile):
    return tile >> 1, pl.ds(pl.multiple_of((tile & 1) * BLK, BLK), BLK)


def by_count(count, most, body):
    for size in range(1, most + 1):
        pl.when(count == size)(functools.partial(body, size))


def order_by_count(live_blocks):
    tiles = live_blocks.shape[0]
    ids = jnp.arange(tiles, dtype=jnp.int32)
    here, there = live_blocks[:, None], live_blocks[None, :]
    ahead = (there > here) | ((there == here) & (ids[None, :] < ids[:, None]))
    rank = jnp.sum(ahead.astype(jnp.int32), axis=1)
    placed = (rank[None, :] == ids[:, None]).astype(jnp.int32)
    return jnp.sum(placed * ids[None, :], axis=1)


def columns_of(ref, head):
    return ref.at[:, pl.ds(head * DH, DH)]


def relay(stages):
    for arrivals, _ in stages:
        for copy in arrivals:
            copy.start()
    for arrivals, departures in stages:
        for copy in arrivals:
            copy.wait()
        for copy in departures:
            copy.start()
    for _, departures in stages:
        for copy in departures:
            copy.wait()


def pack_kernel(array_ref, *refs):
    *tap_refs, out_ref, held_ref, in_sems, out_sems = refs
    rows = array_ref.shape[0]
    stages = []
    for first in range(0, out_ref.shape[0], PACKED):
        heads = pl.ds(first, PACKED)
        arrivals = [
            pltpu.make_async_copy(
                columns_of(array_ref, head), held_ref.at[head, pl.ds(0, rows), :], in_sems.at[head]
            )
            for head in range(first, first + PACKED)
        ]
        for tap_ref in tap_refs:
            arrivals.append(
                pltpu.make_async_copy(
                    tap_ref.at[heads],
                    held_ref.at[heads, pl.ds(rows, tap_ref.shape[1]), :],
                    in_sems.at[out_ref.shape[0] + first // PACKED],
                )
            )
        leaving = pltpu.make_async_copy(
            held_ref.at[heads], out_ref.at[heads], out_sems.at[first // PACKED]
        )
        stages.append((arrivals, [leaving]))
    relay(stages)


def pack(array, *taps):
    rows, width = array.shape
    heads = width // DH
    shape = (heads, rows + sum(tap.shape[1] for tap in taps), DH)
    return pl.pallas_call(
        pack_kernel,
        in_specs=[HBM_SPEC] * (1 + len(taps)),
        out_specs=HBM_SPEC,
        out_shape=jax.ShapeDtypeStruct(shape, array.dtype),
        scratch_shapes=[
            pltpu.VMEM(shape, array.dtype),
            pltpu.SemaphoreType.DMA((heads + heads // PACKED,)),
            pltpu.SemaphoreType.DMA((heads // PACKED,)),
        ],
        compiler_params=pltpu.CompilerParams(vmem_limit_bytes=SMALL_LIMIT),
        cost_estimate=pl.CostEstimate(flops=0, bytes_accessed=4 * rows * width, transcendentals=0),
    )(array, *taps)


def share_sum_kernel(terms_ref, into_ref, out_ref, terms, total, in_sem, out_sems):
    held = total.shape[0]
    rows = out_ref.shape[1] - held
    arrival = pltpu.make_async_copy(terms_ref.at[:, pl.ds(rows, held), :], terms, in_sem)
    arrival.start()
    arrival.wait()
    total[...] = jnp.sum(terms[...].astype(F32), axis=0).astype(BF16)
    copies = [
        pltpu.make_async_copy(total, out_ref.at[device, pl.ds(rows, held), :], out_sems.at[device])
        for device in range(out_ref.shape[0])
    ]
    for copy in copies:
        copy.start()
    for copy in copies:
        copy.wait()


def share_sum(terms, into, held):
    devices = terms.shape[0]
    return pl.pallas_call(
        share_sum_kernel,
        in_specs=[HBM_SPEC] * 2,
        out_specs=HBM_SPEC,
        out_shape=jax.ShapeDtypeStruct(into.shape, into.dtype),
        scratch_shapes=[
            pltpu.VMEM((devices, held, DH), BF16),
            pltpu.VMEM((held, DH), BF16),
            pltpu.SemaphoreType.DMA(()),
            pltpu.SemaphoreType.DMA((devices,)),
        ],
        input_output_aliases={1: 0},
        compiler_params=pltpu.CompilerParams(vmem_limit_bytes=SMALL_LIMIT),
    )(terms, into)


def pack_project_kernel(key_ref, grad_ref, weight_ref, out_ref, sems):
    heads, rows = out_ref.shape[0], key_ref.shape[0]
    copies = [
        pltpu.make_async_copy(
            columns_of(key_ref, head), out_ref.at[head, pl.ds(0, rows), :], sems.at[head]
        )
        for head in range(heads)
    ]
    for copy in copies:
        copy.start()
    for head in range(0, heads, 2):
        projected = lax.dot_general(
            grad_ref[...], weight_ref[head * DH : (head + 2) * DH, :], NT, preferred_element_type=F32
        ).astype(BF16)
        out_ref[head, rows:, :] = projected[:, :DH]
        out_ref[head + 1, rows:, :] = projected[:, DH:]
    for copy in copies:
        copy.wait()


def pack_project(keys, feature_grad, head_weight):
    rows, width = keys.shape
    heads = width // DH
    channels = feature_grad.shape[1]
    return pl.pallas_call(
        pack_project_kernel,
        in_specs=[HBM_SPEC, VMEM_SPEC, VMEM_SPEC],
        out_specs=VMEM_SPEC,
        out_shape=jax.ShapeDtypeStruct((heads, 2 * rows, DH), keys.dtype),
        scratch_shapes=[pltpu.SemaphoreType.DMA((heads,))],
        compiler_params=pltpu.CompilerParams(vmem_limit_bytes=KERNEL_LIMIT),
        cost_estimate=pl.CostEstimate(
            flops=2 * rows * width * channels, bytes_accessed=8 * rows * width, transcendentals=0
        ),
    )(keys, feature_grad, head_weight)


def unpack_kernel(pair_ref, last_ref, *refs):
    *out_refs, held_ref, in_sems, out_sems = refs
    heads, rows = held_ref.shape[0], out_refs[0].shape[0]
    stages = []
    for first in range(0, heads, PACKED):
        group = pl.ds(first, PACKED)
        places = [(pair_ref, 0, 2 * rows), (last_ref, 2 * rows, rows)]
        arrivals = [
            pltpu.make_async_copy(
                ref.at[group, pl.ds(0, length), :],
                held_ref.at[group, pl.ds(start, length), :],
                in_sems.at[place, first // PACKED],
            )
            for place, (ref, start, length) in enumerate(places)
        ]
        departures = [
            pltpu.make_async_copy(
                held_ref.at[head, pl.ds(place * rows, rows), :],
                columns_of(out_ref, head),
                out_sems.at[place, head],
            )
            for head in range(first, first + PACKED)
            for place, out_ref in enumerate(out_refs)
        ]
        stages.append((arrivals, departures))
    relay(stages)


def unpack(pair, last):
    heads, rows = pair.shape[0], pair.shape[1] // 2
    return pl.pallas_call(
        unpack_kernel,
        in_specs=[HBM_SPEC] * 2,
        out_specs=[HBM_SPEC] * 3,
        out_shape=[jax.ShapeDtypeStruct((rows, heads * DH), last.dtype)] * 3,
        scratch_shapes=[
            pltpu.VMEM((heads, 3 * rows, DH), last.dtype),
            pltpu.SemaphoreType.DMA((2, heads // PACKED)),
            pltpu.SemaphoreType.DMA((3, heads)),
        ],
        compiler_params=pltpu.CompilerParams(vmem_limit_bytes=SMALL_LIMIT),
        cost_estimate=pl.CostEstimate(
            flops=0, bytes_accessed=12 * rows * heads * DH, transcendentals=0
        ),
    )(pair, last)


def clear(total_ref):
    def step(block, carry):
        total_ref[block] = jnp.zeros(total_ref.shape[1:], F32)
        return carry

    lax.fori_loop(0, total_ref.shape[0], step, 0)


def gather(ref, blocks, base=0):
    return jnp.concatenate(
        [ref[b >> 1, pl.ds(pl.multiple_of((b & 1) * BLK + base, BLK), BLK), :] for b in blocks], 0
    )


def probs_kernel(
    listed, pattern, live, order, query_ref, key_ref, grad_ref, probs_ref, key_t_ref, out_ref, total_ref
):
    scale = DH ** (-0.5) * math.log2(math.e)
    step, steps = pl.program_id(0), pl.num_programs(0)

    @pl.when(step == 0)
    def _():
        clear(total_ref)

    def group_step(group, carry):
        slots = [group * TOGETHER + t for t in range(TOGETHER)]
        tiles = [order[step * GROUP + slot] for slot in slots]

        def body(size):
            held = []
            for slot, tile in zip(slots, tiles):
                query = query_ref[rows_of(tile)]
                blocks = [pattern[tile * listed + j] for j in range(size)]
                scores = lax.dot_general(
                    gather(key_ref, blocks), query, NT, preferred_element_type=F32
                )
                key_block = lax.broadcasted_iota(jnp.int32, scores.shape, 0) >> 7
                scores = jnp.where(key_block < live[tile], scores, -jnp.inf)
                top = jnp.max(scores, axis=0, keepdims=True)
                weights = jnp.exp2((scores - top) * scale)
                inverse = 1.0 / jnp.sum(weights, axis=0, keepdims=True)
                probs = (weights * inverse).astype(BF16)
                probs_ref[slot, : size * BLK, :] = probs
                terms = jnp.dot(probs, grad_ref[rows_of(tile)], preferred_element_type=F32)
                held.append((blocks, terms))
            for blocks, terms in held:
                for j, b in enumerate(blocks):
                    total_ref[b] += terms[j * BLK : (j + 1) * BLK, :]

        by_count(live[tiles[0]], listed, body)
        for slot in slots:
            key_t_ref[slot] = key_ref[rows_of(step * GROUP + slot)].T
        return carry

    lax.fori_loop(0, GROUP // TOGETHER, group_step, 0)

    @pl.when(step == steps - 1)
    def _():
        def finish(block, carry):
            out_ref[rows_of(block)] = total_ref[block].astype(BF16)
            return carry

        lax.fori_loop(0, total_ref.shape[0], finish, 0)


def whole(shape, index=None):
    index = (0,) * len(shape) if index is None else index
    return pl.BlockSpec(shape, lambda i, *_: index, pipeline_mode=pl.Buffered(1))


def probs_of(query, pair, pattern, live_blocks, order, spare):
    tiles, listed = pattern.shape
    pairs = tiles * listed
    devices, rows, _ = query.shape
    return pl.pallas_call(
        functools.partial(probs_kernel, listed),
        grid_spec=pltpu.PrefetchScalarGridSpec(
            num_scalar_prefetch=3,
            grid=(tiles // GROUP,),
            in_specs=[whole(query.shape), whole(query.shape), whole(query.shape, (0, 1, 0))],
            out_specs=[
                pl.BlockSpec((GROUP, listed * BLK, BLK), lambda i, *_: (i, 0, 0)),
                pl.BlockSpec((GROUP, DH, BLK), lambda i, *_: (i, 0, 0)),
                whole((devices, rows + spare, DH)),
            ],
            scratch_shapes=[pltpu.VMEM((tiles, BLK, DH), F32)],
        ),
        out_shape=[
            jax.ShapeDtypeStruct((tiles, listed * BLK, BLK), BF16),
            jax.ShapeDtypeStruct((tiles, DH, BLK), BF16),
            jax.ShapeDtypeStruct((devices, rows + spare, DH), BF16),
        ],
        compiler_params=pltpu.CompilerParams(vmem_limit_bytes=KERNEL_LIMIT),
        cost_estimate=pl.CostEstimate(
            flops=4 * pairs * BLK * BLK * DH,
            bytes_accessed=2 * pairs * BLK * BLK,
            transcendentals=pairs * BLK * BLK,
        ),
    )(pattern.reshape(-1), live_blocks, order, query, pair, pair)


def grads_kernel(
    listed, pattern, live, order, query_ref, grad_ref, value_ref, key_t_ref, probs_ref, out_ref, total_ref
):
    scale = DH ** (-0.5)
    step, steps = pl.program_id(0), pl.num_programs(0)
    rows = query_ref.shape[1]

    @pl.when(step == 0)
    def _():
        clear(total_ref)

    def group_step(group, carry):
        slots = [group * TOGETHER + t for t in range(TOGETHER)]
        members = [order[step * GROUP + slot] for slot in slots]

        def body(size):
            held = []
            for slot, tile in zip(slots, members):
                blocks = [pattern[tile * listed + j] for j in range(size)]
                dprobs = lax.dot_general(
                    gather(value_ref, blocks), grad_ref[rows_of(tile)], NT, preferred_element_type=F32
                )
                probs = probs_ref[slot, : size * BLK, :].astype(F32)
                delta = jnp.sum(probs * dprobs, axis=0, keepdims=True)
                dscores = (probs * (dprobs - delta)).astype(BF16)
                keys_t = jnp.concatenate([key_t_ref[b] for b in blocks], 1)
                query_grad = jnp.dot(keys_t, dscores, preferred_element_type=F32)
                out_ref[rows_of(tile)] = (query_grad * scale).T.astype(BF16)
                terms = jnp.dot(dscores, query_ref[rows_of(tile)], preferred_element_type=F32)
                held.append((blocks, terms))
            for blocks, terms in held:
                for j, b in enumerate(blocks):
                    total_ref[b] += terms[j * BLK : (j + 1) * BLK, :]

        by_count(live[members[0]], listed, body)
        return carry

    lax.fori_loop(0, GROUP // TOGETHER, group_step, 0)

    @pl.when(step == steps - 1)
    def _():
        def finish(block, carry):
            start = pl.multiple_of((block & 1) * BLK + rows, BLK)
            out_ref[block >> 1, pl.ds(start, BLK), :] = (total_ref[block] * scale).astype(BF16)
            return carry

        lax.fori_loop(0, total_ref.shape[0], finish, 0)


def grads_of(query, pair, values, keys_t, probs, pattern, live_blocks, order):
    tiles, listed = pattern.shape
    pairs = tiles * listed
    devices, rows, _ = query.shape
    return pl.pallas_call(
        functools.partial(grads_kernel, listed),
        grid_spec=pltpu.PrefetchScalarGridSpec(
            num_scalar_prefetch=3,
            grid=(tiles // GROUP,),
            in_specs=[
                whole(query.shape),
                whole(query.shape, (0, 1, 0)),
                whole(query.shape),
                whole(keys_t.shape),
                pl.BlockSpec((GROUP, listed * BLK, BLK), lambda i, *_: (i, 0, 0)),
            ],
            out_specs=whole((devices, 2 * rows, DH)),
            scratch_shapes=[pltpu.VMEM((tiles, BLK, DH), F32)],
        ),
        out_shape=jax.ShapeDtypeStruct((devices, 2 * rows, DH), BF16),
        compiler_params=pltpu.CompilerParams(vmem_limit_bytes=KERNEL_LIMIT),
        cost_estimate=pl.CostEstimate(
            flops=6 * pairs * BLK * BLK * DH,
            bytes_accessed=2 * pairs * BLK * BLK + 16 * tiles * BLK * DH,
            transcendentals=0,
        ),
    )(pattern.reshape(-1), live_blocks, order, query, pair, values, keys_t, probs)


def exchange(blocks):
    return lax.all_to_all(blocks, "ctx", split_axis=0, concat_axis=0, tiled=True)


def body(
    queries, keys, values, features, feat_grad, conv_weight, head_weight, pattern, live_blocks
):
    devices = lax.axis_size("ctx")
    frames, positions, channels = features.shape
    taps = conv_weight.shape[0]
    rows = frames * positions

    incoming = lax.ppermute(feat_grad, "ctx", [(i + 1, i) for i in range(devices - 1)])
    packed = pack(queries)
    packed, incoming, feat_grad = lax.optimization_barrier((packed, incoming, feat_grad))
    query = exchange(packed)

    order = order_by_count(live_blocks)
    extended = jnp.concatenate([feat_grad, incoming], 0)
    windows = [extended[k : k + frames].reshape(rows, channels) for k in range(taps)]
    summed = sum(
        lax.dot_general(windows[k], conv_weight[k], NT, preferred_element_type=F32)
        for k in range(taps)
    )
    flat_features = features.reshape(rows, channels)
    tap_terms = jnp.stack(
        [
            lax.dot_general(flat_features, windows[k], TN, preferred_element_type=F32)
            for k in range(taps)
        ],
        0,
    ).astype(BF16)
    share = tap_terms.size // devices // DH
    held = -(-share // 16) * 16
    tap_terms = jnp.pad(tap_terms.reshape(devices, share, DH), ((0, 0), (0, held - share), (0, 0)))
    pair = pack_project(keys, summed.astype(BF16), head_weight)
    value_taps = pack(values, tap_terms)
    pair, value_taps, query, order = lax.optimization_barrier((pair, value_taps, query, order))

    pair = exchange(pair)
    value_taps, pair = lax.optimization_barrier((value_taps, pair))
    value_taps = exchange(value_taps)
    probs, keys_t, value_grad = probs_of(query, pair, pattern, live_blocks, order, held)

    value_grad = exchange(share_sum(value_taps, value_grad, held))
    grads = grads_of(query, pair, value_taps, keys_t, probs, pattern, live_blocks, order)
    grads, value_grad = lax.optimization_barrier((grads, value_grad))
    grads = exchange(grads)

    grads, value_grad = lax.optimization_barrier((grads, value_grad))
    grad_queries, grad_keys, grad_values = unpack(grads, value_grad)
    tap_total = value_grad[:, rows : rows + share, :].reshape(conv_weight.shape).astype(F32)
    token_count = rows * devices
    conv_weight_grad = tap_total * (1.0 / math.sqrt(token_count))
    return (grad_queries, grad_keys, grad_values, conv_weight_grad)


def solution(mesh):
    placed = (
        P(("clip", "ctx"), None),
        P(("clip", "ctx"), None),
        P(("clip", "ctx"), None),
        P(("clip", "ctx"), None, None),
        P(("clip", "ctx"), None, None),
        P(),
        P(),
        P("clip", None),
        P("clip"),
    )
    return jax.shard_map(
        body,
        mesh=mesh,
        in_specs=placed,
        out_specs=(
            P(("clip", "ctx"), None),
            P(("clip", "ctx"), None),
            P(("clip", "ctx"), None),
            P("clip", None, None),
        ),
        check_vma=False,
    )
```

```python
import functools
import math

import jax
import jax.numpy as jnp
from jax import lax
from jax.experimental import pallas as pl
from jax.experimental.pallas import tpu as pltpu
from jax.sharding import PartitionSpec as P

DH = 128
BLK = 128
TOGETHER = 4
GROUP = 8
PACKED = 4
NT = (((1,), (1,)), ((), ()))
TN = (((0,), (0,)), ((), ()))
F32 = jnp.float32
BF16 = jnp.bfloat16
KERNEL_LIMIT = 56 * 1024 * 1024
SMALL_LIMIT = 16 * 1024 * 1024
MEDIUM_LIMIT = 32 * 1024 * 1024
HBM_SPEC = pl.BlockSpec(memory_space=pl.ANY)
VMEM_SPEC = pl.BlockSpec(memory_space=pltpu.VMEM)


def rows_of(tile):
    return tile >> 1, pl.ds(pl.multiple_of((tile & 1) * BLK, BLK), BLK)


def by_count(count, most, body):
    for size in range(1, most + 1):
        pl.when(count == size)(functools.partial(body, size))


def order_by_count(live_blocks):
    tiles = live_blocks.shape[0]
    ids = jnp.arange(tiles, dtype=jnp.int32)
    here, there = live_blocks[:, None], live_blocks[None, :]
    ahead = (there > here) | ((there == here) & (ids[None, :] < ids[:, None]))
    rank = jnp.sum(ahead.astype(jnp.int32), axis=1)
    placed = (rank[None, :] == ids[:, None]).astype(jnp.int32)
    return jnp.sum(placed * ids[None, :], axis=1)


def in_hbm(array):
    return pltpu.with_memory_space_constraint(array, pltpu.HBM)


def columns_of(ref, head):
    return ref.at[:, pl.ds(head * DH, DH)]


def relay(stages):
    for arrivals, _ in stages:
        for copy in arrivals:
            copy.start()
    for arrivals, departures in stages:
        for copy in arrivals:
            copy.wait()
        for copy in departures:
            copy.start()
    for _, departures in stages:
        for copy in departures:
            copy.wait()


def pack_kernel(query_ref, key_ref, value_ref, triple_ref, last_ref, held_ref, in_sems, out_sems):
    rows = query_ref.shape[0]
    stages = []
    for first in range(0, held_ref.shape[0], PACKED):
        heads = pl.ds(first, PACKED)
        arrivals = [
            pltpu.make_async_copy(
                columns_of(ref, head),
                held_ref.at[head, pl.ds(place * rows, rows), :],
                in_sems.at[place, head],
            )
            for head in range(first, first + PACKED)
            for place, ref in enumerate((query_ref, key_ref, value_ref))
        ]
        departures = [
            pltpu.make_async_copy(
                held_ref.at[heads, pl.ds(0, 2 * rows), :],
                triple_ref.at[heads, pl.ds(0, 2 * rows), :],
                out_sems.at[0, first // PACKED],
            ),
            pltpu.make_async_copy(
                held_ref.at[heads, pl.ds(2 * rows, rows), :],
                last_ref.at[heads, pl.ds(0, rows), :],
                out_sems.at[1, first // PACKED],
            ),
        ]
        stages.append((arrivals, departures))
    relay(stages)


def pack(queries, keys, values, held):
    rows, width = queries.shape
    heads = width // DH
    return pl.pallas_call(
        pack_kernel,
        in_specs=[HBM_SPEC] * 3,
        out_specs=[HBM_SPEC] * 2,
        out_shape=[
            pltpu.HBM((heads, 3 * rows, DH), BF16),
            pltpu.HBM((heads, rows + held, DH), BF16),
        ],
        scratch_shapes=[
            pltpu.VMEM((heads, 3 * rows, DH), BF16),
            pltpu.SemaphoreType.DMA((3, heads)),
            pltpu.SemaphoreType.DMA((2, heads // PACKED)),
        ],
        compiler_params=pltpu.CompilerParams(vmem_limit_bytes=SMALL_LIMIT),
        cost_estimate=pl.CostEstimate(flops=0, bytes_accessed=12 * rows * width, transcendentals=0),
    )(in_hbm(queries), in_hbm(keys), in_hbm(values))


def decoder_kernel(
    near_ref,
    next_ref,
    feature_ref,
    tap_weight_ref,
    head_weight_ref,
    triple_in_ref,
    last_in_ref,
    triple_ref,
    last_ref,
    held_ref,
    taps_ref,
    grad_sems,
    tap_sems,
):
    heads, rows, _ = held_ref.shape
    frames, positions, channels = feature_ref.shape
    devices = last_ref.shape[0]
    share = taps_ref.shape[0] // devices
    steps = [near_ref[f] for f in range(frames)] + [next_ref[f] for f in range(frames)]
    taps = tap_weight_ref.shape[0]
    windows = [jnp.concatenate(steps[k : k + frames], 0) for k in range(taps)]
    feature_grad = sum(
        lax.dot_general(windows[k], tap_weight_ref[k], NT, preferred_element_type=F32)
        for k in range(taps)
    ).astype(BF16)
    copies = []
    for first in range(0, heads, PACKED):
        projected = lax.dot_general(
            feature_grad,
            head_weight_ref[first * DH : (first + PACKED) * DH, :],
            NT,
            preferred_element_type=F32,
        ).astype(BF16)
        for head in range(PACKED):
            held_ref[first + head] = projected[:, head * DH : (head + 1) * DH]
        group = pl.ds(first, PACKED)
        copies.append(
            pltpu.make_async_copy(
                held_ref.at[group],
                triple_ref.at[group, pl.ds(2 * rows, rows), :],
                grad_sems.at[first // PACKED],
            )
        )
        copies[-1].start()
    features_t = jnp.concatenate([feature_ref[f] for f in range(frames)], 0).T
    row = 0
    for k in range(taps):
        terms = jnp.dot(features_t, windows[k], preferred_element_type=F32).astype(BF16)
        for first in range(0, channels, DH):
            taps_ref[row : row + channels, :] = terms[:, first : first + DH]
            row += channels
    taps_ref[row:, :] = jnp.zeros((taps_ref.shape[0] - row, DH), BF16)
    for device in range(devices):
        copies.append(
            pltpu.make_async_copy(
                taps_ref.at[pl.ds(device * share, share), :],
                last_ref.at[device, pl.ds(rows, share), :],
                tap_sems.at[device],
            )
        )
        copies[-1].start()
    for copy in copies:
        copy.wait()


def decoder(feat_grad, incoming, features, conv_weight, head_weight, triple, last):
    heads, rows = triple.shape[0], triple.shape[1] // 3
    share = last.shape[1] - rows
    return pl.pallas_call(
        decoder_kernel,
        in_specs=[VMEM_SPEC] * 5 + [HBM_SPEC] * 2,
        out_specs=[HBM_SPEC] * 2,
        out_shape=[pltpu.HBM(x.shape, x.dtype) for x in (triple, last)],
        scratch_shapes=[
            pltpu.VMEM((heads, rows, DH), BF16),
            pltpu.VMEM((heads * share, DH), BF16),
            pltpu.SemaphoreType.DMA((heads // PACKED,)),
            pltpu.SemaphoreType.DMA((heads,)),
        ],
        input_output_aliases={5: 0, 6: 1},
        compiler_params=pltpu.CompilerParams(vmem_limit_bytes=MEDIUM_LIMIT),
        cost_estimate=pl.CostEstimate(
            flops=2 * heads * rows * DH * head_weight.shape[1],
            bytes_accessed=6 * heads * rows * DH,
            transcendentals=0,
        ),
    )(feat_grad, incoming, features, conv_weight, head_weight, in_hbm(triple), in_hbm(last))


def share_sum_kernel(terms_ref, into_ref, out_ref, terms, total, in_sem, out_sems):
    held = total.shape[0]
    rows = out_ref.shape[1] - held
    arrival = pltpu.make_async_copy(terms_ref.at[:, pl.ds(rows, held), :], terms, in_sem)
    arrival.start()
    arrival.wait()
    total[...] = jnp.sum(terms[...].astype(F32), axis=0).astype(BF16)
    copies = [
        pltpu.make_async_copy(total, out_ref.at[device, pl.ds(rows, held), :], out_sems.at[device])
        for device in range(out_ref.shape[0])
    ]
    for copy in copies:
        copy.start()
    for copy in copies:
        copy.wait()


def share_sum(terms, into, held):
    devices = terms.shape[0]
    return pl.pallas_call(
        share_sum_kernel,
        in_specs=[HBM_SPEC] * 2,
        out_specs=HBM_SPEC,
        out_shape=pltpu.HBM(into.shape, into.dtype),
        scratch_shapes=[
            pltpu.VMEM((devices, held, DH), BF16),
            pltpu.VMEM((held, DH), BF16),
            pltpu.SemaphoreType.DMA(()),
            pltpu.SemaphoreType.DMA((devices,)),
        ],
        input_output_aliases={1: 0},
        compiler_params=pltpu.CompilerParams(vmem_limit_bytes=SMALL_LIMIT),
    )(in_hbm(terms), in_hbm(into))


def unpack_kernel(factor, pair_ref, last_ref, *refs):
    *out_refs, tap_out_ref, held_ref, taps_ref, scaled_ref, in_sems, out_sems, tap_sems, done_sem = refs
    heads, rows = held_ref.shape[0], out_refs[0].shape[0]
    share = last_ref.shape[1] - rows
    tap_copies = [
        pltpu.make_async_copy(
            last_ref.at[device, pl.ds(rows, share), :],
            taps_ref.at[pl.ds(device * share, share), :],
            tap_sems.at[device],
        )
        for device in range(heads)
    ]
    stages = []
    for first in range(0, heads, PACKED):
        group = pl.ds(first, PACKED)
        places = [(pair_ref, 0, 2 * rows), (last_ref, 2 * rows, rows)]
        arrivals = [
            pltpu.make_async_copy(
                ref.at[group, pl.ds(0, length), :],
                held_ref.at[group, pl.ds(start, length), :],
                in_sems.at[place, first // PACKED],
            )
            for place, (ref, start, length) in enumerate(places)
        ]
        departures = [
            pltpu.make_async_copy(
                held_ref.at[head, pl.ds(place * rows, rows), :],
                columns_of(out_ref, head),
                out_sems.at[place, head],
            )
            for head in range(first, first + PACKED)
            for place, out_ref in enumerate(out_refs)
        ]
        stages.append((arrivals, departures))
    for arrivals, _ in stages:
        for copy in arrivals:
            copy.start()
    for copy in tap_copies:
        copy.start()
    for arrivals, departures in stages:
        for copy in arrivals:
            copy.wait()
        for copy in departures:
            copy.start()
    for copy in tap_copies:
        copy.wait()
    taps, channels, width = scaled_ref.shape
    row = 0
    for k in range(taps):
        for first in range(0, width, DH):
            terms = taps_ref[row : row + channels, :].astype(F32) * factor
            scaled_ref[k, :, first : first + DH] = terms
            row += channels
    done = pltpu.make_async_copy(scaled_ref, tap_out_ref, done_sem)
    done.start()
    for _, departures in stages:
        for copy in departures:
            copy.wait()
    done.wait()


def unpack(pair, last, tap_shape, factor):
    heads, rows = pair.shape[0], pair.shape[1] // 2
    return pl.pallas_call(
        functools.partial(unpack_kernel, factor),
        in_specs=[HBM_SPEC] * 2,
        out_specs=[HBM_SPEC] * 4,
        out_shape=[jax.ShapeDtypeStruct((rows, heads * DH), last.dtype)] * 3
        + [jax.ShapeDtypeStruct(tap_shape, F32)],
        scratch_shapes=[
            pltpu.VMEM((heads, 3 * rows, DH), last.dtype),
            pltpu.VMEM((heads * (last.shape[1] - rows), DH), last.dtype),
            pltpu.VMEM(tap_shape, F32),
            pltpu.SemaphoreType.DMA((2, heads // PACKED)),
            pltpu.SemaphoreType.DMA((3, heads)),
            pltpu.SemaphoreType.DMA((heads,)),
            pltpu.SemaphoreType.DMA(()),
        ],
        compiler_params=pltpu.CompilerParams(vmem_limit_bytes=SMALL_LIMIT),
        cost_estimate=pl.CostEstimate(
            flops=0, bytes_accessed=12 * rows * heads * DH, transcendentals=0
        ),
    )(in_hbm(pair), in_hbm(last))


def clear(total_ref):
    def step(block, carry):
        total_ref[block] = jnp.zeros(total_ref.shape[1:], F32)
        return carry

    lax.fori_loop(0, total_ref.shape[0], step, 0)


def gather(ref, blocks, base=0):
    return jnp.concatenate(
        [ref[b >> 1, pl.ds(pl.multiple_of((b & 1) * BLK + base, BLK), BLK), :] for b in blocks], 0
    )


def probs_kernel(
    listed, pattern, live, order, query_ref, key_ref, grad_ref, probs_ref, key_t_ref, out_ref, total_ref
):
    scale = DH ** (-0.5) * math.log2(math.e)
    step, steps = pl.program_id(0), pl.num_programs(0)

    @pl.when(step == 0)
    def _():
        clear(total_ref)

    def group_step(group, carry):
        slots = [group * TOGETHER + t for t in range(TOGETHER)]
        tiles = [order[step * GROUP + slot] for slot in slots]

        def body(size):
            held = []
            for slot, tile in zip(slots, tiles):
                query = query_ref[rows_of(tile)]
                blocks = [pattern[tile * listed + j] for j in range(size)]
                scores = lax.dot_general(
                    gather(key_ref, blocks), query, NT, preferred_element_type=F32
                )
                key_block = lax.broadcasted_iota(jnp.int32, scores.shape, 0) >> 7
                scores = jnp.where(key_block < live[tile], scores, -jnp.inf)
                top = jnp.max(scores, axis=0, keepdims=True)
                weights = jnp.exp2((scores - top) * scale)
                inverse = 1.0 / jnp.sum(weights, axis=0, keepdims=True)
                probs = (weights * inverse).astype(BF16)
                probs_ref[slot, : size * BLK, :] = probs
                terms = jnp.dot(probs, grad_ref[rows_of(tile)], preferred_element_type=F32)
                held.append((blocks, terms))
            for blocks, terms in held:
                for j, b in enumerate(blocks):
                    total_ref[b] += terms[j * BLK : (j + 1) * BLK, :]

        by_count(live[tiles[0]], listed, body)
        for slot in slots:
            key_t_ref[slot] = key_ref[rows_of(step * GROUP + slot)].T
        return carry

    lax.fori_loop(0, GROUP // TOGETHER, group_step, 0)

    @pl.when(step == steps - 1)
    def _():
        def finish(block, carry):
            out_ref[rows_of(block)] = total_ref[block].astype(BF16)
            return carry

        lax.fori_loop(0, total_ref.shape[0], finish, 0)


def whole(shape, index=None):
    index = (0,) * len(shape) if index is None else index
    return pl.BlockSpec(shape, lambda i, *_: index, pipeline_mode=pl.Buffered(1))


def probs_of(triple, pattern, live_blocks, order, spare):
    tiles, listed = pattern.shape
    pairs = tiles * listed
    devices, rows = triple.shape[0], triple.shape[1] // 3
    part = (devices, rows, DH)
    return pl.pallas_call(
        functools.partial(probs_kernel, listed),
        grid_spec=pltpu.PrefetchScalarGridSpec(
            num_scalar_prefetch=3,
            grid=(tiles // GROUP,),
            in_specs=[whole(part, (0, place, 0)) for place in range(3)],
            out_specs=[
                pl.BlockSpec((GROUP, listed * BLK, BLK), lambda i, *_: (i, 0, 0)),
                pl.BlockSpec((GROUP, DH, BLK), lambda i, *_: (i, 0, 0)),
                whole((devices, rows + spare, DH)),
            ],
            scratch_shapes=[pltpu.VMEM((tiles, BLK, DH), F32)],
        ),
        out_shape=[
            jax.ShapeDtypeStruct((tiles, listed * BLK, BLK), BF16),
            jax.ShapeDtypeStruct((tiles, DH, BLK), BF16),
            pltpu.HBM((devices, rows + spare, DH), BF16),
        ],
        compiler_params=pltpu.CompilerParams(vmem_limit_bytes=KERNEL_LIMIT),
        cost_estimate=pl.CostEstimate(
            flops=4 * pairs * BLK * BLK * DH,
            bytes_accessed=2 * pairs * BLK * BLK,
            transcendentals=pairs * BLK * BLK,
        ),
    )(pattern.reshape(-1), live_blocks, order, triple, triple, triple)


def grads_kernel(
    listed, pattern, live, order, query_ref, grad_ref, value_ref, key_t_ref, probs_ref, out_ref, total_ref
):
    scale = DH ** (-0.5)
    step, steps = pl.program_id(0), pl.num_programs(0)
    rows = query_ref.shape[1]

    @pl.when(step == 0)
    def _():
        clear(total_ref)

    def group_step(group, carry):
        slots = [group * TOGETHER + t for t in range(TOGETHER)]
        members = [order[step * GROUP + slot] for slot in slots]

        def body(size):
            held = []
            for slot, tile in zip(slots, members):
                blocks = [pattern[tile * listed + j] for j in range(size)]
                dprobs = lax.dot_general(
                    gather(value_ref, blocks), grad_ref[rows_of(tile)], NT, preferred_element_type=F32
                )
                probs = probs_ref[slot, : size * BLK, :].astype(F32)
                delta = jnp.sum(probs * dprobs, axis=0, keepdims=True)
                dscores = (probs * (dprobs - delta)).astype(BF16)
                keys_t = jnp.concatenate([key_t_ref[b] for b in blocks], 1)
                query_grad = jnp.dot(keys_t, dscores, preferred_element_type=F32)
                out_ref[rows_of(tile)] = (query_grad * scale).T.astype(BF16)
                terms = jnp.dot(dscores, query_ref[rows_of(tile)], preferred_element_type=F32)
                held.append((blocks, terms))
            for blocks, terms in held:
                for j, b in enumerate(blocks):
                    total_ref[b] += terms[j * BLK : (j + 1) * BLK, :]

        by_count(live[members[0]], listed, body)
        return carry

    lax.fori_loop(0, GROUP // TOGETHER, group_step, 0)

    @pl.when(step == steps - 1)
    def _():
        def finish(block, carry):
            start = pl.multiple_of((block & 1) * BLK + rows, BLK)
            out_ref[block >> 1, pl.ds(start, BLK), :] = (total_ref[block] * scale).astype(BF16)
            return carry

        lax.fori_loop(0, total_ref.shape[0], finish, 0)


def grads_of(triple, values, keys_t, probs, pattern, live_blocks, order):
    tiles, listed = pattern.shape
    pairs = tiles * listed
    devices, rows = triple.shape[0], triple.shape[1] // 3
    part = (devices, rows, DH)
    return pl.pallas_call(
        functools.partial(grads_kernel, listed),
        grid_spec=pltpu.PrefetchScalarGridSpec(
            num_scalar_prefetch=3,
            grid=(tiles // GROUP,),
            in_specs=[
                whole(part),
                whole(part, (0, 2, 0)),
                whole(part),
                whole(keys_t.shape),
                pl.BlockSpec((GROUP, listed * BLK, BLK), lambda i, *_: (i, 0, 0)),
            ],
            out_specs=whole((devices, 2 * rows, DH)),
            scratch_shapes=[pltpu.VMEM((tiles, BLK, DH), F32)],
        ),
        out_shape=jax.ShapeDtypeStruct((devices, 2 * rows, DH), BF16),
        compiler_params=pltpu.CompilerParams(vmem_limit_bytes=KERNEL_LIMIT),
        cost_estimate=pl.CostEstimate(
            flops=6 * pairs * BLK * BLK * DH,
            bytes_accessed=2 * pairs * BLK * BLK + 16 * tiles * BLK * DH,
            transcendentals=0,
        ),
    )(pattern.reshape(-1), live_blocks, order, triple, triple, values, keys_t, probs)


def exchange(blocks):
    return lax.all_to_all(blocks, "ctx", split_axis=0, concat_axis=0, tiled=True)


def body(
    queries, keys, values, features, feat_grad, conv_weight, head_weight, pattern, live_blocks
):
    devices = lax.axis_size("ctx")
    frames, positions, channels = features.shape
    rows = frames * positions
    share = -(-conv_weight.size // devices // DH // 16) * 16

    incoming = lax.ppermute(feat_grad, "ctx", [(i + 1, i) for i in range(devices - 1)])
    order = order_by_count(live_blocks)
    triple, value_taps = pack(queries, keys, values, share)
    triple, value_taps, order, incoming = lax.optimization_barrier(
        (triple, value_taps, order, incoming)
    )
    triple, value_taps = decoder(
        feat_grad, incoming, features, conv_weight, head_weight, triple, value_taps
    )

    triple = exchange(triple)
    value_taps, triple = lax.optimization_barrier((value_taps, triple))
    value_taps = exchange(value_taps)
    probs, keys_t, value_grad = probs_of(triple, pattern, live_blocks, order, share)

    value_grad = exchange(share_sum(value_taps, value_grad, share))
    grads = grads_of(triple, value_taps, keys_t, probs, pattern, live_blocks, order)
    grads, value_grad = lax.optimization_barrier((grads, value_grad))
    grads = exchange(grads)

    factor = 1.0 / math.sqrt(rows * devices)
    return tuple(unpack(grads, value_grad, conv_weight.shape, factor))


def solution(mesh):
    placed = (
        P(("clip", "ctx"), None),
        P(("clip", "ctx"), None),
        P(("clip", "ctx"), None),
        P(("clip", "ctx"), None, None),
        P(("clip", "ctx"), None, None),
        P(),
        P(),
        P("clip", None),
        P("clip"),
    )
    return jax.shard_map(
        body,
        mesh=mesh,
        in_specs=placed,
        out_specs=(
            P(("clip", "ctx"), None),
            P(("clip", "ctx"), None),
            P(("clip", "ctx"), None),
            P("clip", None, None),
        ),
        check_vma=False,
    )
```

```python
import functools
import math

import jax
import jax.numpy as jnp
from jax import lax
from jax.experimental import pallas as pl
from jax.experimental.pallas import tpu as pltpu
from jax.sharding import PartitionSpec as P

DH = 128
BLK = 128
TOGETHER = 4
GROUP = 8
PACKED = 4
NT = (((1,), (1,)), ((), ()))
TN = (((0,), (0,)), ((), ()))
F32 = jnp.float32
BF16 = jnp.bfloat16
KERNEL_LIMIT = 56 * 1024 * 1024
SMALL_LIMIT = 16 * 1024 * 1024
MEDIUM_LIMIT = 32 * 1024 * 1024
HBM_SPEC = pl.BlockSpec(memory_space=pl.ANY)
VMEM_SPEC = pl.BlockSpec(memory_space=pltpu.VMEM)


def rows_of(tile):
    return tile >> 1, pl.ds(pl.multiple_of((tile & 1) * BLK, BLK), BLK)


def by_count(count, most, body):
    for size in range(1, most + 1):
        pl.when(count == size)(functools.partial(body, size))


def order_by_count(live_blocks):
    tiles = live_blocks.shape[0]
    ids = jnp.arange(tiles, dtype=jnp.int32)
    here, there = live_blocks[:, None], live_blocks[None, :]
    ahead = (there > here) | ((there == here) & (ids[None, :] < ids[:, None]))
    rank = jnp.sum(ahead.astype(jnp.int32), axis=1)
    placed = (rank[None, :] == ids[:, None]).astype(jnp.int32)
    return jnp.sum(placed * ids[None, :], axis=1)


def in_hbm(array):
    return pltpu.with_memory_space_constraint(array, pltpu.HBM)


def columns_of(ref, head):
    return ref.at[:, pl.ds(head * DH, DH)]


def relay(stages):
    for arrivals, _ in stages:
        for copy in arrivals:
            copy.start()
    for arrivals, departures in stages:
        for copy in arrivals:
            copy.wait()
        for copy in departures:
            copy.start()
    for _, departures in stages:
        for copy in departures:
            copy.wait()


def pack_kernel(query_ref, key_ref, value_ref, triple_ref, last_ref, held_ref, in_sems, out_sems):
    rows = query_ref.shape[0]
    stages = []
    for first in range(0, held_ref.shape[0], PACKED):
        heads = pl.ds(first, PACKED)
        arrivals = [
            pltpu.make_async_copy(
                columns_of(ref, head),
                held_ref.at[head, pl.ds(place * rows, rows), :],
                in_sems.at[place, head],
            )
            for head in range(first, first + PACKED)
            for place, ref in enumerate((query_ref, key_ref, value_ref))
        ]
        departures = [
            pltpu.make_async_copy(
                held_ref.at[heads, pl.ds(0, 2 * rows), :],
                triple_ref.at[heads, pl.ds(0, 2 * rows), :],
                out_sems.at[0, first // PACKED],
            ),
            pltpu.make_async_copy(
                held_ref.at[heads, pl.ds(2 * rows, rows), :],
                last_ref.at[heads],
                out_sems.at[1, first // PACKED],
            ),
        ]
        stages.append((arrivals, departures))
    relay(stages)


def pack(queries, keys, values):
    rows, width = queries.shape
    heads = width // DH
    return pl.pallas_call(
        pack_kernel,
        in_specs=[HBM_SPEC] * 3,
        out_specs=[HBM_SPEC] * 2,
        out_shape=[
            pltpu.HBM((heads, 3 * rows, DH), BF16),
            pltpu.HBM((heads, rows, DH), BF16),
        ],
        scratch_shapes=[
            pltpu.VMEM((heads, 3 * rows, DH), BF16),
            pltpu.SemaphoreType.DMA((3, heads)),
            pltpu.SemaphoreType.DMA((2, heads // PACKED)),
        ],
        compiler_params=pltpu.CompilerParams(vmem_limit_bytes=SMALL_LIMIT),
        cost_estimate=pl.CostEstimate(flops=0, bytes_accessed=12 * rows * width, transcendentals=0),
    )(in_hbm(queries), in_hbm(keys), in_hbm(values))


def decoder_kernel(
    near_ref,
    next_ref,
    feature_ref,
    tap_weight_ref,
    head_weight_ref,
    triple_in_ref,
    triple_ref,
    taps_ref,
    held_ref,
    grad_sems,
):
    heads, rows, _ = held_ref.shape
    frames, positions, channels = feature_ref.shape
    steps = [near_ref[f] for f in range(frames)] + [next_ref[f] for f in range(frames)]
    taps = tap_weight_ref.shape[0]
    windows = [jnp.concatenate(steps[k : k + frames], 0) for k in range(taps)]
    feature_grad = sum(
        lax.dot_general(windows[k], tap_weight_ref[k], NT, preferred_element_type=F32)
        for k in range(taps)
    ).astype(BF16)
    copies = []
    for first in range(0, heads, PACKED):
        projected = lax.dot_general(
            feature_grad,
            head_weight_ref[first * DH : (first + PACKED) * DH, :],
            NT,
            preferred_element_type=F32,
        ).astype(BF16)
        for head in range(PACKED):
            held_ref[first + head] = projected[:, head * DH : (head + 1) * DH]
        group = pl.ds(first, PACKED)
        copies.append(
            pltpu.make_async_copy(
                held_ref.at[group],
                triple_ref.at[group, pl.ds(2 * rows, rows), :],
                grad_sems.at[first // PACKED],
            )
        )
        copies[-1].start()
    features_t = jnp.concatenate([feature_ref[f] for f in range(frames)], 0).T
    row = 0
    for k in range(taps):
        terms = jnp.dot(features_t, windows[k], preferred_element_type=F32).astype(BF16)
        for first in range(0, channels, DH):
            taps_ref[row : row + channels, :] = terms[:, first : first + DH]
            row += channels
    for copy in copies:
        copy.wait()


def decoder(feat_grad, incoming, features, conv_weight, head_weight, triple):
    heads, rows = triple.shape[0], triple.shape[1] // 3
    return pl.pallas_call(
        decoder_kernel,
        in_specs=[VMEM_SPEC] * 5 + [HBM_SPEC],
        out_specs=[HBM_SPEC, VMEM_SPEC],
        out_shape=[
            pltpu.HBM(triple.shape, triple.dtype),
            jax.ShapeDtypeStruct((conv_weight.size // DH, DH), BF16),
        ],
        scratch_shapes=[
            pltpu.VMEM((heads, rows, DH), BF16),
            pltpu.SemaphoreType.DMA((heads // PACKED,)),
        ],
        input_output_aliases={5: 0},
        compiler_params=pltpu.CompilerParams(vmem_limit_bytes=MEDIUM_LIMIT),
        cost_estimate=pl.CostEstimate(
            flops=2 * heads * rows * DH * head_weight.shape[1],
            bytes_accessed=6 * heads * rows * DH,
            transcendentals=0,
        ),
    )(feat_grad, incoming, features, conv_weight, head_weight, in_hbm(triple))


def unpack_kernel(factor, pair_ref, last_ref, sums_ref, *refs):
    *out_refs, tap_out_ref, held_ref, taps_ref, scaled_ref, in_sems, out_sems, tap_sems = refs
    heads, rows = held_ref.shape[0], out_refs[0].shape[0]
    tap_copy = pltpu.make_async_copy(sums_ref, taps_ref, tap_sems.at[0])
    tap_copy.start()
    stages = []
    for first in range(0, heads, PACKED):
        group = pl.ds(first, PACKED)
        places = [(pair_ref, 0, 2 * rows), (last_ref, 2 * rows, rows)]
        arrivals = [
            pltpu.make_async_copy(
                ref.at[group, pl.ds(0, length), :],
                held_ref.at[group, pl.ds(start, length), :],
                in_sems.at[place, first // PACKED],
            )
            for place, (ref, start, length) in enumerate(places)
        ]
        departures = [
            pltpu.make_async_copy(
                held_ref.at[head, pl.ds(place * rows, rows), :],
                columns_of(out_ref, head),
                out_sems.at[place, head],
            )
            for head in range(first, first + PACKED)
            for place, out_ref in enumerate(out_refs)
        ]
        stages.append((arrivals, departures))
    for arrivals, _ in stages:
        for copy in arrivals:
            copy.start()
    for arrivals, departures in stages:
        for copy in arrivals:
            copy.wait()
        for copy in departures:
            copy.start()
    tap_copy.wait()
    taps, channels, width = scaled_ref.shape
    row = 0
    for k in range(taps):
        for first in range(0, width, DH):
            terms = taps_ref[row : row + channels, :].astype(F32) * factor
            scaled_ref[k, :, first : first + DH] = terms
            row += channels
    done = pltpu.make_async_copy(scaled_ref, tap_out_ref, tap_sems.at[1])
    done.start()
    for _, departures in stages:
        for copy in departures:
            copy.wait()
    done.wait()


def unpack(pair, last, sums, tap_shape, factor):
    heads, rows = pair.shape[0], pair.shape[1] // 2
    return pl.pallas_call(
        functools.partial(unpack_kernel, factor),
        in_specs=[HBM_SPEC] * 3,
        out_specs=[HBM_SPEC] * 4,
        out_shape=[jax.ShapeDtypeStruct((rows, heads * DH), last.dtype)] * 3
        + [jax.ShapeDtypeStruct(tap_shape, F32)],
        scratch_shapes=[
            pltpu.VMEM((heads, 3 * rows, DH), last.dtype),
            pltpu.VMEM(sums.shape, sums.dtype),
            pltpu.VMEM(tap_shape, F32),
            pltpu.SemaphoreType.DMA((2, heads // PACKED)),
            pltpu.SemaphoreType.DMA((3, heads)),
            pltpu.SemaphoreType.DMA((2,)),
        ],
        compiler_params=pltpu.CompilerParams(vmem_limit_bytes=SMALL_LIMIT),
        cost_estimate=pl.CostEstimate(
            flops=0, bytes_accessed=12 * rows * heads * DH, transcendentals=0
        ),
    )(in_hbm(pair), in_hbm(last), in_hbm(sums))


def clear(total_ref):
    def step(block, carry):
        total_ref[block] = jnp.zeros(total_ref.shape[1:], F32)
        return carry

    lax.fori_loop(0, total_ref.shape[0], step, 0)


def gather(ref, blocks, base=0):
    return jnp.concatenate(
        [ref[b >> 1, pl.ds(pl.multiple_of((b & 1) * BLK + base, BLK), BLK), :] for b in blocks], 0
    )


def probs_kernel(
    listed, pattern, live, order, query_ref, key_ref, grad_ref, probs_ref, key_t_ref, out_ref, total_ref
):
    scale = DH ** (-0.5) * math.log2(math.e)
    step, steps = pl.program_id(0), pl.num_programs(0)

    @pl.when(step == 0)
    def _():
        clear(total_ref)

    def group_step(group, carry):
        slots = [group * TOGETHER + t for t in range(TOGETHER)]
        tiles = [order[step * GROUP + slot] for slot in slots]

        def body(size):
            held = []
            for slot, tile in zip(slots, tiles):
                query = query_ref[rows_of(tile)]
                blocks = [pattern[tile * listed + j] for j in range(size)]
                scores = lax.dot_general(
                    gather(key_ref, blocks), query, NT, preferred_element_type=F32
                )
                key_block = lax.broadcasted_iota(jnp.int32, scores.shape, 0) >> 7
                scores = jnp.where(key_block < live[tile], scores, -jnp.inf)
                top = jnp.max(scores, axis=0, keepdims=True)
                weights = jnp.exp2((scores - top) * scale)
                inverse = 1.0 / jnp.sum(weights, axis=0, keepdims=True)
                probs = (weights * inverse).astype(BF16)
                probs_ref[slot, : size * BLK, :] = probs
                terms = jnp.dot(probs, grad_ref[rows_of(tile)], preferred_element_type=F32)
                held.append((blocks, terms))
            for blocks, terms in held:
                for j, b in enumerate(blocks):
                    total_ref[b] += terms[j * BLK : (j + 1) * BLK, :]

        by_count(live[tiles[0]], listed, body)
        for slot in slots:
            key_t_ref[slot] = key_ref[rows_of(step * GROUP + slot)].T
        return carry

    lax.fori_loop(0, GROUP // TOGETHER, group_step, 0)

    @pl.when(step == steps - 1)
    def _():
        def finish(block, carry):
            out_ref[rows_of(block)] = total_ref[block].astype(BF16)
            return carry

        lax.fori_loop(0, total_ref.shape[0], finish, 0)


def whole(shape, index=None):
    index = (0,) * len(shape) if index is None else index
    return pl.BlockSpec(shape, lambda i, *_: index, pipeline_mode=pl.Buffered(1))


def probs_of(triple, pattern, live_blocks, order):
    tiles, listed = pattern.shape
    pairs = tiles * listed
    devices, rows = triple.shape[0], triple.shape[1] // 3
    part = (devices, rows, DH)
    return pl.pallas_call(
        functools.partial(probs_kernel, listed),
        grid_spec=pltpu.PrefetchScalarGridSpec(
            num_scalar_prefetch=3,
            grid=(tiles // GROUP,),
            in_specs=[whole(part, (0, place, 0)) for place in range(3)],
            out_specs=[
                pl.BlockSpec((GROUP, listed * BLK, BLK), lambda i, *_: (i, 0, 0)),
                pl.BlockSpec((GROUP, DH, BLK), lambda i, *_: (i, 0, 0)),
                whole(part),
            ],
            scratch_shapes=[pltpu.VMEM((tiles, BLK, DH), F32)],
        ),
        out_shape=[
            jax.ShapeDtypeStruct((tiles, listed * BLK, BLK), BF16),
            jax.ShapeDtypeStruct((tiles, DH, BLK), BF16),
            pltpu.HBM(part, BF16),
        ],
        compiler_params=pltpu.CompilerParams(vmem_limit_bytes=KERNEL_LIMIT),
        cost_estimate=pl.CostEstimate(
            flops=4 * pairs * BLK * BLK * DH,
            bytes_accessed=2 * pairs * BLK * BLK,
            transcendentals=pairs * BLK * BLK,
        ),
    )(pattern.reshape(-1), live_blocks, order, triple, triple, triple)


def grads_kernel(
    listed, pattern, live, order, query_ref, grad_ref, value_ref, key_t_ref, probs_ref, out_ref, total_ref
):
    scale = DH ** (-0.5)
    step, steps = pl.program_id(0), pl.num_programs(0)
    rows = query_ref.shape[1]

    @pl.when(step == 0)
    def _():
        clear(total_ref)

    def group_step(group, carry):
        slots = [group * TOGETHER + t for t in range(TOGETHER)]
        members = [order[step * GROUP + slot] for slot in slots]

        def body(size):
            held = []
            for slot, tile in zip(slots, members):
                blocks = [pattern[tile * listed + j] for j in range(size)]
                dprobs = lax.dot_general(
                    gather(value_ref, blocks), grad_ref[rows_of(tile)], NT, preferred_element_type=F32
                )
                probs = probs_ref[slot, : size * BLK, :].astype(F32)
                delta = jnp.sum(probs * dprobs, axis=0, keepdims=True)
                dscores = (probs * (dprobs - delta)).astype(BF16)
                keys_t = jnp.concatenate([key_t_ref[b] for b in blocks], 1)
                query_grad = jnp.dot(keys_t, dscores, preferred_element_type=F32)
                out_ref[rows_of(tile)] = (query_grad * scale).T.astype(BF16)
                terms = jnp.dot(dscores, query_ref[rows_of(tile)], preferred_element_type=F32)
                held.append((blocks, terms))
            for blocks, terms in held:
                for j, b in enumerate(blocks):
                    total_ref[b] += terms[j * BLK : (j + 1) * BLK, :]

        by_count(live[members[0]], listed, body)
        return carry

    lax.fori_loop(0, GROUP // TOGETHER, group_step, 0)

    @pl.when(step == steps - 1)
    def _():
        def finish(block, carry):
            start = pl.multiple_of((block & 1) * BLK + rows, BLK)
            out_ref[block >> 1, pl.ds(start, BLK), :] = (total_ref[block] * scale).astype(BF16)
            return carry

        lax.fori_loop(0, total_ref.shape[0], finish, 0)


def grads_of(triple, values, keys_t, probs, pattern, live_blocks, order):
    tiles, listed = pattern.shape
    pairs = tiles * listed
    devices, rows = triple.shape[0], triple.shape[1] // 3
    part = (devices, rows, DH)
    return pl.pallas_call(
        functools.partial(grads_kernel, listed),
        grid_spec=pltpu.PrefetchScalarGridSpec(
            num_scalar_prefetch=3,
            grid=(tiles // GROUP,),
            in_specs=[
                whole(part),
                whole(part, (0, 2, 0)),
                whole(part),
                whole(keys_t.shape),
                pl.BlockSpec((GROUP, listed * BLK, BLK), lambda i, *_: (i, 0, 0)),
            ],
            out_specs=whole((devices, 2 * rows, DH)),
            scratch_shapes=[pltpu.VMEM((tiles, BLK, DH), F32)],
        ),
        out_shape=jax.ShapeDtypeStruct((devices, 2 * rows, DH), BF16),
        compiler_params=pltpu.CompilerParams(vmem_limit_bytes=KERNEL_LIMIT),
        cost_estimate=pl.CostEstimate(
            flops=6 * pairs * BLK * BLK * DH,
            bytes_accessed=2 * pairs * BLK * BLK + 16 * tiles * BLK * DH,
            transcendentals=0,
        ),
    )(pattern.reshape(-1), live_blocks, order, triple, triple, values, keys_t, probs)


def exchange(blocks):
    return lax.all_to_all(blocks, "ctx", split_axis=0, concat_axis=0, tiled=True)


def tap_groups(devices):
    count = devices // 8
    fours = [[8 * a + 2 * b + c for b in range(4)] for a in range(count) for c in range(2)]
    pairs = [[2 * a, 2 * a + 1] for a in range(devices // 2)]
    eights = [[8 * a + b for a in range(count)] for b in range(8)]
    return fours, pairs, eights


def body(
    queries, keys, values, features, feat_grad, conv_weight, head_weight, pattern, live_blocks
):
    devices = lax.axis_size("ctx")
    frames, positions, channels = features.shape
    rows = frames * positions

    incoming = lax.ppermute(feat_grad, "ctx", [(i + 1, i) for i in range(devices - 1)])
    order = order_by_count(live_blocks)
    triple, values = pack(queries, keys, values)
    triple, values, order, incoming = lax.optimization_barrier((triple, values, order, incoming))
    triple, sums = decoder(feat_grad, incoming, features, conv_weight, head_weight, triple)
    first, second, third = tap_groups(devices)
    sums = lax.psum(sums, "ctx", axis_index_groups=first)

    triple = exchange(triple)
    values, triple, sums = lax.optimization_barrier((values, triple, sums))
    sums = lax.psum(sums, "ctx", axis_index_groups=second)
    values = exchange(values)
    probs, keys_t, value_grad = probs_of(triple, pattern, live_blocks, order)

    value_grad, values = lax.optimization_barrier((value_grad, values))
    value_grad = exchange(value_grad)
    grads = grads_of(triple, values, keys_t, probs, pattern, live_blocks, order)
    grads, value_grad, sums = lax.optimization_barrier((grads, value_grad, sums))
    sums = lax.psum(sums, "ctx", axis_index_groups=third)
    grads = exchange(grads)

    factor = 1.0 / math.sqrt(rows * devices)
    return tuple(unpack(grads, value_grad, sums, conv_weight.shape, factor))


def solution(mesh):
    placed = (
        P(("clip", "ctx"), None),
        P(("clip", "ctx"), None),
        P(("clip", "ctx"), None),
        P(("clip", "ctx"), None, None),
        P(("clip", "ctx"), None, None),
        P(),
        P(),
        P("clip", None),
        P("clip"),
    )
    return jax.shard_map(
        body,
        mesh=mesh,
        in_specs=placed,
        out_specs=(
            P(("clip", "ctx"), None),
            P(("clip", "ctx"), None),
            P(("clip", "ctx"), None),
            P("clip", None, None),
        ),
        check_vma=False,
    )
```

```python
import functools
import math

import jax
import jax.numpy as jnp
from jax import lax
from jax.experimental import pallas as pl
from jax.experimental.pallas import tpu as pltpu
from jax.sharding import PartitionSpec as P

DH = 128
BLK = 128
TOGETHER = 4
GROUP = 8
PACKED = 4
NT = (((1,), (1,)), ((), ()))
TN = (((0,), (0,)), ((), ()))
F32 = jnp.float32
BF16 = jnp.bfloat16
KERNEL_LIMIT = 56 * 1024 * 1024
SMALL_LIMIT = 16 * 1024 * 1024
MEDIUM_LIMIT = 32 * 1024 * 1024
HBM_SPEC = pl.BlockSpec(memory_space=pl.ANY)
VMEM_SPEC = pl.BlockSpec(memory_space=pltpu.VMEM)


def rows_of(tile):
    return tile >> 1, pl.ds(pl.multiple_of((tile & 1) * BLK, BLK), BLK)


def by_count(count, most, body):
    for size in range(1, most + 1):
        pl.when(count == size)(functools.partial(body, size))


def order_by_count(live_blocks):
    tiles = live_blocks.shape[0]
    ids = jnp.arange(tiles, dtype=jnp.int32)
    here, there = live_blocks[:, None], live_blocks[None, :]
    ahead = (there > here) | ((there == here) & (ids[None, :] < ids[:, None]))
    rank = jnp.sum(ahead.astype(jnp.int32), axis=1)
    placed = (rank[None, :] == ids[:, None]).astype(jnp.int32)
    return jnp.sum(placed * ids[None, :], axis=1)


def in_hbm(array):
    return pltpu.with_memory_space_constraint(array, pltpu.HBM)


def columns_of(ref, head):
    return ref.at[:, pl.ds(head * DH, DH)]


def pack_kernel(query_ref, key_ref, value_ref, triple_ref, last_ref, held_ref, in_sems, out_sems):
    rows = query_ref.shape[0]
    arrivals = [
        pltpu.make_async_copy(ref, held_ref.at[place], in_sems.at[place])
        for place, ref in enumerate((query_ref, key_ref, value_ref))
    ]
    for copy in arrivals:
        copy.start()
    departures = []
    for place, arrival in enumerate(arrivals):
        arrival.wait()
        for head in range(triple_ref.shape[0]):
            source = held_ref.at[place, :, pl.ds(head * DH, DH)]
            if place < 2:
                target = triple_ref.at[head, pl.ds(place * rows, rows), :]
            else:
                target = last_ref.at[head, pl.ds(0, rows), :]
            departures.append(pltpu.make_async_copy(source, target, out_sems.at[place, head]))
            departures[-1].start()
    for copy in departures:
        copy.wait()


def pack(queries, keys, values, held):
    rows, width = queries.shape
    heads = width // DH
    return pl.pallas_call(
        pack_kernel,
        in_specs=[HBM_SPEC] * 3,
        out_specs=[HBM_SPEC] * 2,
        out_shape=[
            pltpu.HBM((heads, 3 * rows, DH), BF16),
            pltpu.HBM((heads, rows + held, DH), BF16),
        ],
        scratch_shapes=[
            pltpu.VMEM((3, rows, width), BF16),
            pltpu.SemaphoreType.DMA((3,)),
            pltpu.SemaphoreType.DMA((3, heads)),
        ],
        compiler_params=pltpu.CompilerParams(vmem_limit_bytes=SMALL_LIMIT),
        cost_estimate=pl.CostEstimate(flops=0, bytes_accessed=12 * rows * width, transcendentals=0),
    )(in_hbm(queries), in_hbm(keys), in_hbm(values))


def decoder_kernel(
    near_ref,
    next_ref,
    feature_ref,
    tap_weight_ref,
    head_weight_ref,
    triple_in_ref,
    last_in_ref,
    triple_ref,
    last_ref,
    held_ref,
    taps_ref,
    grad_sems,
    tap_sems,
):
    heads, rows, _ = held_ref.shape
    frames, positions, channels = feature_ref.shape
    devices = last_ref.shape[0]
    share = taps_ref.shape[0] // devices
    steps = [near_ref[f] for f in range(frames)] + [next_ref[f] for f in range(frames)]
    taps = tap_weight_ref.shape[0]
    windows = [jnp.concatenate(steps[k : k + frames], 0) for k in range(taps)]
    feature_grad = sum(
        lax.dot_general(windows[k], tap_weight_ref[k], NT, preferred_element_type=F32)
        for k in range(taps)
    ).astype(BF16)
    copies = []
    for first in range(0, heads, PACKED):
        projected = lax.dot_general(
            feature_grad,
            head_weight_ref[first * DH : (first + PACKED) * DH, :],
            NT,
            preferred_element_type=F32,
        ).astype(BF16)
        for head in range(PACKED):
            held_ref[first + head] = projected[:, head * DH : (head + 1) * DH]
        group = pl.ds(first, PACKED)
        copies.append(
            pltpu.make_async_copy(
                held_ref.at[group],
                triple_ref.at[group, pl.ds(2 * rows, rows), :],
                grad_sems.at[first // PACKED],
            )
        )
        copies[-1].start()
    features_t = jnp.concatenate([feature_ref[f] for f in range(frames)], 0).T
    row = 0
    for k in range(taps):
        terms = jnp.dot(features_t, windows[k], preferred_element_type=F32).astype(BF16)
        for first in range(0, channels, DH):
            taps_ref[row : row + channels, :] = terms[:, first : first + DH]
            row += channels
    taps_ref[row:, :] = jnp.zeros((taps_ref.shape[0] - row, DH), BF16)
    for device in range(devices):
        copies.append(
            pltpu.make_async_copy(
                taps_ref.at[pl.ds(device * share, share), :],
                last_ref.at[device, pl.ds(rows, share), :],
                tap_sems.at[device],
            )
        )
        copies[-1].start()
    for copy in copies:
        copy.wait()


def decoder(feat_grad, incoming, features, conv_weight, head_weight, triple, last):
    heads, rows = triple.shape[0], triple.shape[1] // 3
    share = last.shape[1] - rows
    return pl.pallas_call(
        decoder_kernel,
        in_specs=[VMEM_SPEC] * 5 + [HBM_SPEC] * 2,
        out_specs=[HBM_SPEC] * 2,
        out_shape=[pltpu.HBM(x.shape, x.dtype) for x in (triple, last)],
        scratch_shapes=[
            pltpu.VMEM((heads, rows, DH), BF16),
            pltpu.VMEM((heads * share, DH), BF16),
            pltpu.SemaphoreType.DMA((heads // PACKED,)),
            pltpu.SemaphoreType.DMA((heads,)),
        ],
        input_output_aliases={5: 0, 6: 1},
        compiler_params=pltpu.CompilerParams(vmem_limit_bytes=MEDIUM_LIMIT),
        cost_estimate=pl.CostEstimate(
            flops=2 * heads * rows * DH * head_weight.shape[1],
            bytes_accessed=6 * heads * rows * DH,
            transcendentals=0,
        ),
    )(feat_grad, incoming, features, conv_weight, head_weight, in_hbm(triple), in_hbm(last))


def share_sum_kernel(terms_ref, into_ref, out_ref, total, sems):
    held = total.shape[0]
    rows = out_ref.shape[1] - held
    total[...] = jnp.sum(terms_ref[:, rows:, :].astype(F32), axis=0).astype(BF16)
    copies = [
        pltpu.make_async_copy(total, out_ref.at[device, pl.ds(rows, held), :], sems.at[device])
        for device in range(out_ref.shape[0])
    ]
    for copy in copies:
        copy.start()
    for copy in copies:
        copy.wait()


def share_sum(terms, into, held):
    devices = terms.shape[0]
    return pl.pallas_call(
        share_sum_kernel,
        in_specs=[VMEM_SPEC, HBM_SPEC],
        out_specs=HBM_SPEC,
        out_shape=pltpu.HBM(into.shape, into.dtype),
        scratch_shapes=[
            pltpu.VMEM((held, DH), BF16),
            pltpu.SemaphoreType.DMA((devices,)),
        ],
        input_output_aliases={1: 0},
        compiler_params=pltpu.CompilerParams(vmem_limit_bytes=SMALL_LIMIT),
    )(terms, in_hbm(into))


def unpack_kernel(factor, pair_ref, last_ref, *refs):
    *out_refs, tap_out_ref, held_ref, taps_ref, scaled_ref, in_sems, out_sems, done_sem = refs
    heads, rows = held_ref.shape[0], out_refs[0].shape[0]
    share = last_ref.shape[1] - rows
    arrivals = []
    for first in range(0, heads, PACKED):
        group = pl.ds(first, PACKED)
        arrivals.append(
            pltpu.make_async_copy(
                pair_ref.at[group], held_ref.at[group], in_sems.at[first // PACKED]
            )
        )
        arrivals[-1].start()
    departures = []
    for head in range(heads):
        source = last_ref.at[head, pl.ds(0, rows), :]
        departures.append(
            pltpu.make_async_copy(source, columns_of(out_refs[2], head), out_sems.at[2, head])
        )
        departures[-1].start()
    for head in range(heads):
        taps_ref[head * share : (head + 1) * share, :] = last_ref[head, rows:, :]
    taps, channels, width = scaled_ref.shape
    row = 0
    for k in range(taps):
        for first in range(0, width, DH):
            terms = taps_ref[row : row + channels, :].astype(F32) * factor
            scaled_ref[k, :, first : first + DH] = terms
            row += channels
    departures.append(pltpu.make_async_copy(scaled_ref, tap_out_ref, done_sem))
    departures[-1].start()
    for place, arrival in enumerate(arrivals):
        arrival.wait()
        for head in range(place * PACKED, (place + 1) * PACKED):
            for part in range(2):
                source = held_ref.at[head, pl.ds(part * rows, rows), :]
                departures.append(
                    pltpu.make_async_copy(
                        source, columns_of(out_refs[part], head), out_sems.at[part, head]
                    )
                )
                departures[-1].start()
    for copy in departures:
        copy.wait()


def unpack(pair, last, tap_shape, factor):
    heads, rows = pair.shape[0], pair.shape[1] // 2
    return pl.pallas_call(
        functools.partial(unpack_kernel, factor),
        in_specs=[HBM_SPEC, VMEM_SPEC],
        out_specs=[HBM_SPEC] * 4,
        out_shape=[jax.ShapeDtypeStruct((rows, heads * DH), last.dtype)] * 3
        + [jax.ShapeDtypeStruct(tap_shape, F32)],
        scratch_shapes=[
            pltpu.VMEM((heads, 2 * rows, DH), last.dtype),
            pltpu.VMEM((heads * (last.shape[1] - rows), DH), last.dtype),
            pltpu.VMEM(tap_shape, F32),
            pltpu.SemaphoreType.DMA((heads // PACKED,)),
            pltpu.SemaphoreType.DMA((3, heads)),
            pltpu.SemaphoreType.DMA(()),
        ],
        compiler_params=pltpu.CompilerParams(vmem_limit_bytes=SMALL_LIMIT),
        cost_estimate=pl.CostEstimate(
            flops=0, bytes_accessed=12 * rows * heads * DH, transcendentals=0
        ),
    )(in_hbm(pair), last)


def clear(total_ref):
    def step(block, carry):
        total_ref[block] = jnp.zeros(total_ref.shape[1:], F32)
        return carry

    lax.fori_loop(0, total_ref.shape[0], step, 0)


def gather(ref, blocks, base=0):
    return jnp.concatenate(
        [ref[b >> 1, pl.ds(pl.multiple_of((b & 1) * BLK + base, BLK), BLK), :] for b in blocks], 0
    )


def probs_kernel(
    listed, pattern, live, order, query_ref, key_ref, grad_ref, probs_ref, key_t_ref, out_ref, total_ref
):
    scale = DH ** (-0.5) * math.log2(math.e)
    step, steps = pl.program_id(0), pl.num_programs(0)

    @pl.when(step == 0)
    def _():
        clear(total_ref)

    def group_step(group, carry):
        slots = [group * TOGETHER + t for t in range(TOGETHER)]
        tiles = [order[step * GROUP + slot] for slot in slots]

        def body(size):
            held = []
            for slot, tile in zip(slots, tiles):
                query = query_ref[rows_of(tile)]
                blocks = [pattern[tile * listed + j] for j in range(size)]
                scores = lax.dot_general(
                    gather(key_ref, blocks), query, NT, preferred_element_type=F32
                )
                key_block = lax.broadcasted_iota(jnp.int32, scores.shape, 0) >> 7
                scores = jnp.where(key_block < live[tile], scores, -jnp.inf)
                top = jnp.max(scores, axis=0, keepdims=True)
                weights = jnp.exp2((scores - top) * scale)
                inverse = 1.0 / jnp.sum(weights, axis=0, keepdims=True)
                probs = (weights * inverse).astype(BF16)
                probs_ref[slot, : size * BLK, :] = probs
                terms = jnp.dot(probs, grad_ref[rows_of(tile)], preferred_element_type=F32)
                held.append((blocks, terms))
            for blocks, terms in held:
                for j, b in enumerate(blocks):
                    total_ref[b] += terms[j * BLK : (j + 1) * BLK, :]

        by_count(live[tiles[0]], listed, body)
        for slot in slots:
            key_t_ref[slot] = key_ref[rows_of(step * GROUP + slot)].T
        return carry

    lax.fori_loop(0, GROUP // TOGETHER, group_step, 0)

    @pl.when(step == steps - 1)
    def _():
        def finish(block, carry):
            out_ref[rows_of(block)] = total_ref[block].astype(BF16)
            return carry

        lax.fori_loop(0, total_ref.shape[0], finish, 0)


def whole(shape, index=None):
    index = (0,) * len(shape) if index is None else index
    return pl.BlockSpec(shape, lambda i, *_: index, pipeline_mode=pl.Buffered(1))


def probs_of(triple, pattern, live_blocks, order, spare):
    tiles, listed = pattern.shape
    pairs = tiles * listed
    devices, rows = triple.shape[0], triple.shape[1] // 3
    part = (devices, rows, DH)
    return pl.pallas_call(
        functools.partial(probs_kernel, listed),
        grid_spec=pltpu.PrefetchScalarGridSpec(
            num_scalar_prefetch=3,
            grid=(tiles // GROUP,),
            in_specs=[whole(part, (0, place, 0)) for place in range(3)],
            out_specs=[
                pl.BlockSpec((GROUP, listed * BLK, BLK), lambda i, *_: (i, 0, 0)),
                pl.BlockSpec((GROUP, DH, BLK), lambda i, *_: (i, 0, 0)),
                whole((devices, rows + spare, DH)),
            ],
            scratch_shapes=[pltpu.VMEM((tiles, BLK, DH), F32)],
        ),
        out_shape=[
            jax.ShapeDtypeStruct((tiles, listed * BLK, BLK), BF16),
            jax.ShapeDtypeStruct((tiles, DH, BLK), BF16),
            pltpu.HBM((devices, rows + spare, DH), BF16),
        ],
        compiler_params=pltpu.CompilerParams(vmem_limit_bytes=KERNEL_LIMIT),
        cost_estimate=pl.CostEstimate(
            flops=4 * pairs * BLK * BLK * DH,
            bytes_accessed=2 * pairs * BLK * BLK,
            transcendentals=pairs * BLK * BLK,
        ),
    )(pattern.reshape(-1), live_blocks, order, triple, triple, triple)


def grads_kernel(
    listed, pattern, live, order, query_ref, grad_ref, value_ref, key_t_ref, probs_ref, out_ref, total_ref
):
    scale = DH ** (-0.5)
    step, steps = pl.program_id(0), pl.num_programs(0)
    rows = query_ref.shape[1]

    @pl.when(step == 0)
    def _():
        clear(total_ref)

    def group_step(group, carry):
        slots = [group * TOGETHER + t for t in range(TOGETHER)]
        members = [order[step * GROUP + slot] for slot in slots]

        def body(size):
            held = []
            for slot, tile in zip(slots, members):
                blocks = [pattern[tile * listed + j] for j in range(size)]
                dprobs = lax.dot_general(
                    gather(value_ref, blocks), grad_ref[rows_of(tile)], NT, preferred_element_type=F32
                )
                probs = probs_ref[slot, : size * BLK, :].astype(F32)
                delta = jnp.sum(probs * dprobs, axis=0, keepdims=True)
                dscores = (probs * (dprobs - delta)).astype(BF16)
                keys_t = jnp.concatenate([key_t_ref[b] for b in blocks], 1)
                query_grad = jnp.dot(keys_t, dscores, preferred_element_type=F32)
                out_ref[rows_of(tile)] = (query_grad * scale).T.astype(BF16)
                terms = jnp.dot(dscores, query_ref[rows_of(tile)], preferred_element_type=F32)
                held.append((blocks, terms))
            for blocks, terms in held:
                for j, b in enumerate(blocks):
                    total_ref[b] += terms[j * BLK : (j + 1) * BLK, :]

        by_count(live[members[0]], listed, body)
        return carry

    lax.fori_loop(0, GROUP // TOGETHER, group_step, 0)

    @pl.when(step == steps - 1)
    def _():
        def finish(block, carry):
            start = pl.multiple_of((block & 1) * BLK + rows, BLK)
            out_ref[block >> 1, pl.ds(start, BLK), :] = (total_ref[block] * scale).astype(BF16)
            return carry

        lax.fori_loop(0, total_ref.shape[0], finish, 0)


def grads_of(triple, values, keys_t, probs, pattern, live_blocks, order):
    tiles, listed = pattern.shape
    pairs = tiles * listed
    devices, rows = triple.shape[0], triple.shape[1] // 3
    part = (devices, rows, DH)
    return pl.pallas_call(
        functools.partial(grads_kernel, listed),
        grid_spec=pltpu.PrefetchScalarGridSpec(
            num_scalar_prefetch=3,
            grid=(tiles // GROUP,),
            in_specs=[
                whole(part),
                whole(part, (0, 2, 0)),
                whole(part),
                whole(keys_t.shape),
                pl.BlockSpec((GROUP, listed * BLK, BLK), lambda i, *_: (i, 0, 0)),
            ],
            out_specs=whole((devices, 2 * rows, DH)),
            scratch_shapes=[pltpu.VMEM((tiles, BLK, DH), F32)],
        ),
        out_shape=jax.ShapeDtypeStruct((devices, 2 * rows, DH), BF16),
        compiler_params=pltpu.CompilerParams(vmem_limit_bytes=KERNEL_LIMIT),
        cost_estimate=pl.CostEstimate(
            flops=6 * pairs * BLK * BLK * DH,
            bytes_accessed=2 * pairs * BLK * BLK + 16 * tiles * BLK * DH,
            transcendentals=0,
        ),
    )(pattern.reshape(-1), live_blocks, order, triple, triple, values, keys_t, probs)


def exchange(blocks):
    return lax.all_to_all(blocks, "ctx", split_axis=0, concat_axis=0, tiled=True)


def body(
    queries, keys, values, features, feat_grad, conv_weight, head_weight, pattern, live_blocks
):
    devices = lax.axis_size("ctx")
    frames, positions, channels = features.shape
    rows = frames * positions
    share = -(-conv_weight.size // devices // DH // 16) * 16

    incoming = lax.ppermute(feat_grad, "ctx", [(i + 1, i) for i in range(devices - 1)])
    order = order_by_count(live_blocks)
    triple, value_taps = pack(queries, keys, values, share)
    triple, value_taps, order, incoming = lax.optimization_barrier(
        (triple, value_taps, order, incoming)
    )
    triple, value_taps = decoder(
        feat_grad, incoming, features, conv_weight, head_weight, triple, value_taps
    )

    triple = exchange(triple)
    value_taps, triple = lax.optimization_barrier((value_taps, triple))
    value_taps = exchange(value_taps)
    probs, keys_t, value_grad = probs_of(triple, pattern, live_blocks, order, share)

    value_grad = exchange(share_sum(value_taps, value_grad, share))
    grads = grads_of(triple, value_taps, keys_t, probs, pattern, live_blocks, order)
    grads, value_grad = lax.optimization_barrier((grads, value_grad))
    grads = exchange(grads)

    factor = 1.0 / math.sqrt(rows * devices)
    return tuple(unpack(grads, value_grad, conv_weight.shape, factor))


def solution(mesh):
    placed = (
        P(("clip", "ctx"), None),
        P(("clip", "ctx"), None),
        P(("clip", "ctx"), None),
        P(("clip", "ctx"), None, None),
        P(("clip", "ctx"), None, None),
        P(),
        P(),
        P("clip", None),
        P("clip"),
    )
    return jax.shard_map(
        body,
        mesh=mesh,
        in_specs=placed,
        out_specs=(
            P(("clip", "ctx"), None),
            P(("clip", "ctx"), None),
            P(("clip", "ctx"), None),
            P("clip", None, None),
        ),
        check_vma=False,
    )
```

```python
import functools
import math

import jax
import jax.numpy as jnp
from jax import lax
from jax.experimental import pallas as pl
from jax.experimental.pallas import tpu as pltpu
from jax.sharding import PartitionSpec as P

DH = 128
BLK = 128
TOGETHER = 4
PROBS_TOGETHER = 8
GROUP = 8
PACKED = 4
NT = (((1,), (1,)), ((), ()))
TN = (((0,), (0,)), ((), ()))
F32 = jnp.float32
BF16 = jnp.bfloat16
KERNEL_LIMIT = 56 * 1024 * 1024
SMALL_LIMIT = 16 * 1024 * 1024
MEDIUM_LIMIT = 32 * 1024 * 1024
HBM_SPEC = pl.BlockSpec(memory_space=pl.ANY)
VMEM_SPEC = pl.BlockSpec(memory_space=pltpu.VMEM)


def rows_of(tile):
    return tile >> 1, pl.ds(pl.multiple_of((tile & 1) * BLK, BLK), BLK)


def by_count(count, most, body):
    for size in range(1, most + 1):
        pl.when(count == size)(functools.partial(body, size))


def order_by_count(live_blocks):
    tiles = live_blocks.shape[0]
    ids = jnp.arange(tiles, dtype=jnp.int32)
    here, there = live_blocks[:, None], live_blocks[None, :]
    ahead = (there > here) | ((there == here) & (ids[None, :] < ids[:, None]))
    rank = jnp.sum(ahead.astype(jnp.int32), axis=1)
    placed = (rank[None, :] == ids[:, None]).astype(jnp.int32)
    return jnp.sum(placed * ids[None, :], axis=1)


def in_hbm(array):
    return pltpu.with_memory_space_constraint(array, pltpu.HBM)


def columns_of(ref, head):
    return ref.at[:, pl.ds(head * DH, DH)]


def pack_kernel(query_ref, key_ref, value_ref, triple_ref, last_ref, held_ref, in_sems, out_sems):
    rows = query_ref.shape[0]
    arrivals = [
        pltpu.make_async_copy(ref, held_ref.at[place], in_sems.at[place])
        for place, ref in enumerate((query_ref, key_ref, value_ref))
    ]
    for copy in arrivals:
        copy.start()
    departures = []
    for place, arrival in enumerate(arrivals):
        arrival.wait()
        for head in range(triple_ref.shape[0]):
            source = held_ref.at[place, :, pl.ds(head * DH, DH)]
            if place < 2:
                target = triple_ref.at[head, pl.ds(place * rows, rows), :]
            else:
                target = last_ref.at[head]
            departures.append(pltpu.make_async_copy(source, target, out_sems.at[place, head]))
            departures[-1].start()
    for copy in departures:
        copy.wait()


def pack(queries, keys, values, held):
    rows, width = queries.shape
    heads = width // DH
    return pl.pallas_call(
        pack_kernel,
        in_specs=[HBM_SPEC] * 3,
        out_specs=[HBM_SPEC] * 2,
        out_shape=[
            pltpu.HBM((heads, 3 * rows + held, DH), BF16),
            pltpu.HBM((heads, rows, DH), BF16),
        ],
        scratch_shapes=[
            pltpu.VMEM((3, rows, width), BF16),
            pltpu.SemaphoreType.DMA((3,)),
            pltpu.SemaphoreType.DMA((3, heads)),
        ],
        compiler_params=pltpu.CompilerParams(vmem_limit_bytes=SMALL_LIMIT),
        cost_estimate=pl.CostEstimate(flops=0, bytes_accessed=12 * rows * width, transcendentals=0),
    )(in_hbm(queries), in_hbm(keys), in_hbm(values))


def decoder_kernel(
    near_ref,
    next_ref,
    feature_ref,
    tap_weight_ref,
    head_weight_ref,
    triple_in_ref,
    triple_ref,
    held_ref,
    taps_ref,
    grad_sems,
    tap_sems,
):
    heads, rows, _ = held_ref.shape
    frames, positions, channels = feature_ref.shape
    devices = triple_ref.shape[0]
    share = taps_ref.shape[0] // devices
    steps = [near_ref[f] for f in range(frames)] + [next_ref[f] for f in range(frames)]
    taps = tap_weight_ref.shape[0]
    windows = [jnp.concatenate(steps[k : k + frames], 0) for k in range(taps)]
    feature_grad = sum(
        lax.dot_general(windows[k], tap_weight_ref[k], NT, preferred_element_type=F32)
        for k in range(taps)
    ).astype(BF16)
    copies = []
    for first in range(0, heads, PACKED):
        projected = lax.dot_general(
            feature_grad,
            head_weight_ref[first * DH : (first + PACKED) * DH, :],
            NT,
            preferred_element_type=F32,
        ).astype(BF16)
        for head in range(PACKED):
            held_ref[first + head] = projected[:, head * DH : (head + 1) * DH]
        group = pl.ds(first, PACKED)
        copies.append(
            pltpu.make_async_copy(
                held_ref.at[group],
                triple_ref.at[group, pl.ds(2 * rows, rows), :],
                grad_sems.at[first // PACKED],
            )
        )
        copies[-1].start()
    features_t = jnp.concatenate([feature_ref[f] for f in range(frames)], 0).T
    row = 0
    for k in range(taps):
        terms = jnp.dot(features_t, windows[k], preferred_element_type=F32).astype(BF16)
        for first in range(0, channels, DH):
            taps_ref[row : row + channels, :] = terms[:, first : first + DH]
            row += channels
    taps_ref[row:, :] = jnp.zeros((taps_ref.shape[0] - row, DH), BF16)
    for device in range(devices):
        copies.append(
            pltpu.make_async_copy(
                taps_ref.at[pl.ds(device * share, share), :],
                triple_ref.at[device, pl.ds(3 * rows, share), :],
                tap_sems.at[device],
            )
        )
        copies[-1].start()
    for copy in copies:
        copy.wait()


def decoder(feat_grad, incoming, features, conv_weight, head_weight, triple):
    heads, rows = triple.shape[0], features.shape[0] * features.shape[1]
    share = triple.shape[1] - 3 * rows
    return pl.pallas_call(
        decoder_kernel,
        in_specs=[VMEM_SPEC] * 5 + [HBM_SPEC],
        out_specs=HBM_SPEC,
        out_shape=pltpu.HBM(triple.shape, triple.dtype),
        scratch_shapes=[
            pltpu.VMEM((heads, rows, DH), BF16),
            pltpu.VMEM((heads * share, DH), BF16),
            pltpu.SemaphoreType.DMA((heads // PACKED,)),
            pltpu.SemaphoreType.DMA((heads,)),
        ],
        input_output_aliases={5: 0},
        compiler_params=pltpu.CompilerParams(vmem_limit_bytes=MEDIUM_LIMIT),
        cost_estimate=pl.CostEstimate(
            flops=2 * heads * rows * DH * head_weight.shape[1],
            bytes_accessed=6 * heads * rows * DH,
            transcendentals=0,
        ),
    )(feat_grad, incoming, features, conv_weight, head_weight, in_hbm(triple))


def share_sum_kernel(terms_ref, into_ref, out_ref, terms, total, in_sem, out_sems):
    held = total.shape[0]
    rows = out_ref.shape[1] - held
    first = terms_ref.shape[1] - held
    arrival = pltpu.make_async_copy(terms_ref.at[:, pl.ds(first, held), :], terms, in_sem)
    arrival.start()
    arrival.wait()
    total[...] = jnp.sum(terms[...].astype(F32), axis=0).astype(BF16)
    copies = [
        pltpu.make_async_copy(total, out_ref.at[device, pl.ds(rows, held), :], out_sems.at[device])
        for device in range(out_ref.shape[0])
    ]
    for copy in copies:
        copy.start()
    for copy in copies:
        copy.wait()


def share_sum(terms, into, held):
    devices = terms.shape[0]
    return pl.pallas_call(
        share_sum_kernel,
        in_specs=[HBM_SPEC] * 2,
        out_specs=HBM_SPEC,
        out_shape=pltpu.HBM(into.shape, into.dtype),
        scratch_shapes=[
            pltpu.VMEM((devices, held, DH), BF16),
            pltpu.VMEM((held, DH), BF16),
            pltpu.SemaphoreType.DMA(()),
            pltpu.SemaphoreType.DMA((devices,)),
        ],
        input_output_aliases={1: 0},
        compiler_params=pltpu.CompilerParams(vmem_limit_bytes=SMALL_LIMIT),
    )(in_hbm(terms), in_hbm(into))


def unpack_kernel(factor, pair_ref, last_ref, *refs):
    *out_refs, tap_out_ref, taps_ref, scaled_ref, out_sems, done_sem = refs
    heads, rows = pair_ref.shape[0], out_refs[0].shape[0]
    share = last_ref.shape[1] - rows
    departures = []
    for part, (ref, start) in enumerate([(pair_ref, 0), (pair_ref, rows), (last_ref, 0)]):
        for head in range(heads):
            source = ref.at[head, pl.ds(start, rows), :]
            departures.append(
                pltpu.make_async_copy(
                    source, columns_of(out_refs[part], head), out_sems.at[part, head]
                )
            )
            departures[-1].start()
    for head in range(heads):
        taps_ref[head * share : (head + 1) * share, :] = last_ref[head, rows:, :]
    taps, channels, width = scaled_ref.shape
    row = 0
    for k in range(taps):
        for first in range(0, width, DH):
            terms = taps_ref[row : row + channels, :].astype(F32) * factor
            scaled_ref[k, :, first : first + DH] = terms
            row += channels
    departures.append(pltpu.make_async_copy(scaled_ref, tap_out_ref, done_sem))
    departures[-1].start()
    for copy in departures:
        copy.wait()


def unpack(pair, last, tap_shape, factor):
    heads, rows = pair.shape[0], pair.shape[1] // 2
    return pl.pallas_call(
        functools.partial(unpack_kernel, factor),
        in_specs=[VMEM_SPEC] * 2,
        out_specs=[HBM_SPEC] * 4,
        out_shape=[jax.ShapeDtypeStruct((rows, heads * DH), last.dtype)] * 3
        + [jax.ShapeDtypeStruct(tap_shape, F32)],
        scratch_shapes=[
            pltpu.VMEM((heads * (last.shape[1] - rows), DH), last.dtype),
            pltpu.VMEM(tap_shape, F32),
            pltpu.SemaphoreType.DMA((3, heads)),
            pltpu.SemaphoreType.DMA(()),
        ],
        compiler_params=pltpu.CompilerParams(vmem_limit_bytes=SMALL_LIMIT),
        cost_estimate=pl.CostEstimate(
            flops=0, bytes_accessed=12 * rows * heads * DH, transcendentals=0
        ),
    )(pair, last)


def clear(total_ref):
    def step(block, carry):
        total_ref[block] = jnp.zeros(total_ref.shape[1:], F32)
        return carry

    lax.fori_loop(0, total_ref.shape[0], step, 0)


def gather(ref, blocks, base=0):
    return jnp.concatenate(
        [ref[b >> 1, pl.ds(pl.multiple_of((b & 1) * BLK + base, BLK), BLK), :] for b in blocks], 0
    )


def probs_kernel(
    listed, pattern, live, order, query_ref, key_ref, grad_ref, probs_ref, key_t_ref, out_ref, total_ref
):
    scale = DH ** (-0.5) * math.log2(math.e)
    step, steps = pl.program_id(0), pl.num_programs(0)

    @pl.when(step == 0)
    def _():
        clear(total_ref)

    def group_step(group, carry):
        slots = [group * PROBS_TOGETHER + t for t in range(PROBS_TOGETHER)]
        tiles = [order[step * GROUP + slot] for slot in slots]

        def body(size):
            held = []
            for slot, tile in zip(slots, tiles):
                query = query_ref[rows_of(tile)]
                blocks = [pattern[tile * listed + j] for j in range(size)]
                scores = lax.dot_general(
                    gather(key_ref, blocks), query, NT, preferred_element_type=F32
                )
                key_block = lax.broadcasted_iota(jnp.int32, scores.shape, 0) >> 7
                scores = jnp.where(key_block < live[tile], scores, -jnp.inf)
                top = jnp.max(scores, axis=0, keepdims=True)
                weights = jnp.exp2((scores - top) * scale)
                inverse = 1.0 / jnp.sum(weights, axis=0, keepdims=True)
                probs = (weights * inverse).astype(BF16)
                probs_ref[slot, : size * BLK, :] = probs
                terms = jnp.dot(probs, grad_ref[rows_of(tile)], preferred_element_type=F32)
                held.append((blocks, terms))
            for blocks, terms in held:
                for j, b in enumerate(blocks):
                    total_ref[b] += terms[j * BLK : (j + 1) * BLK, :]

        by_count(live[tiles[0]], listed, body)
        for slot in slots:
            key_t_ref[slot] = key_ref[rows_of(step * GROUP + slot)].T
        return carry

    lax.fori_loop(0, GROUP // PROBS_TOGETHER, group_step, 0)

    @pl.when(step == steps - 1)
    def _():
        def finish(block, carry):
            out_ref[rows_of(block)] = total_ref[block].astype(BF16)
            return carry

        lax.fori_loop(0, total_ref.shape[0], finish, 0)


def whole(shape, index=None):
    index = (0,) * len(shape) if index is None else index
    return pl.BlockSpec(shape, lambda i, *_: index, pipeline_mode=pl.Buffered(1))


def probs_of(triple, rows, pattern, live_blocks, order, spare):
    tiles, listed = pattern.shape
    pairs = tiles * listed
    devices = triple.shape[0]
    part = (devices, rows, DH)
    return pl.pallas_call(
        functools.partial(probs_kernel, listed),
        grid_spec=pltpu.PrefetchScalarGridSpec(
            num_scalar_prefetch=3,
            grid=(tiles // GROUP,),
            in_specs=[whole(part, (0, place, 0)) for place in range(3)],
            out_specs=[
                pl.BlockSpec((GROUP, listed * BLK, BLK), lambda i, *_: (i, 0, 0)),
                pl.BlockSpec((GROUP, DH, BLK), lambda i, *_: (i, 0, 0)),
                whole((devices, rows + spare, DH)),
            ],
            scratch_shapes=[pltpu.VMEM((tiles, BLK, DH), F32)],
        ),
        out_shape=[
            jax.ShapeDtypeStruct((tiles, listed * BLK, BLK), BF16),
            jax.ShapeDtypeStruct((tiles, DH, BLK), BF16),
            pltpu.HBM((devices, rows + spare, DH), BF16),
        ],
        compiler_params=pltpu.CompilerParams(vmem_limit_bytes=KERNEL_LIMIT),
        cost_estimate=pl.CostEstimate(
            flops=4 * pairs * BLK * BLK * DH,
            bytes_accessed=2 * pairs * BLK * BLK,
            transcendentals=pairs * BLK * BLK,
        ),
    )(pattern.reshape(-1), live_blocks, order, triple, triple, triple)


def grads_kernel(
    listed, pattern, live, order, query_ref, grad_ref, value_ref, key_t_ref, probs_ref, out_ref, total_ref
):
    scale = DH ** (-0.5)
    step, steps = pl.program_id(0), pl.num_programs(0)
    rows = query_ref.shape[1]

    @pl.when(step == 0)
    def _():
        clear(total_ref)

    def group_step(group, carry):
        slots = [group * TOGETHER + t for t in range(TOGETHER)]
        members = [order[step * GROUP + slot] for slot in slots]

        def body(size):
            held = []
            for slot, tile in zip(slots, members):
                blocks = [pattern[tile * listed + j] for j in range(size)]
                dprobs = lax.dot_general(
                    gather(value_ref, blocks), grad_ref[rows_of(tile)], NT, preferred_element_type=F32
                )
                probs = probs_ref[slot, : size * BLK, :].astype(F32)
                delta = jnp.sum(probs * dprobs, axis=0, keepdims=True)
                dscores = (probs * (dprobs - delta)).astype(BF16)
                keys_t = jnp.concatenate([key_t_ref[b] for b in blocks], 1)
                query_grad = jnp.dot(keys_t, dscores, preferred_element_type=F32)
                out_ref[rows_of(tile)] = (query_grad * scale).T.astype(BF16)
                terms = jnp.dot(dscores, query_ref[rows_of(tile)], preferred_element_type=F32)
                held.append((blocks, terms))
            for blocks, terms in held:
                for j, b in enumerate(blocks):
                    total_ref[b] += terms[j * BLK : (j + 1) * BLK, :]

        by_count(live[members[0]], listed, body)
        return carry

    lax.fori_loop(0, GROUP // TOGETHER, group_step, 0)

    @pl.when(step == steps - 1)
    def _():
        def finish(block, carry):
            start = pl.multiple_of((block & 1) * BLK + rows, BLK)
            out_ref[block >> 1, pl.ds(start, BLK), :] = (total_ref[block] * scale).astype(BF16)
            return carry

        lax.fori_loop(0, total_ref.shape[0], finish, 0)


def grads_of(triple, rows, values, keys_t, probs, pattern, live_blocks, order):
    tiles, listed = pattern.shape
    pairs = tiles * listed
    devices = triple.shape[0]
    part = (devices, rows, DH)
    return pl.pallas_call(
        functools.partial(grads_kernel, listed),
        grid_spec=pltpu.PrefetchScalarGridSpec(
            num_scalar_prefetch=3,
            grid=(tiles // GROUP,),
            in_specs=[
                whole(part),
                whole(part, (0, 2, 0)),
                whole(part),
                whole(keys_t.shape),
                pl.BlockSpec((GROUP, listed * BLK, BLK), lambda i, *_: (i, 0, 0)),
            ],
            out_specs=whole((devices, 2 * rows, DH)),
            scratch_shapes=[pltpu.VMEM((tiles, BLK, DH), F32)],
        ),
        out_shape=jax.ShapeDtypeStruct((devices, 2 * rows, DH), BF16),
        compiler_params=pltpu.CompilerParams(vmem_limit_bytes=KERNEL_LIMIT),
        cost_estimate=pl.CostEstimate(
            flops=6 * pairs * BLK * BLK * DH,
            bytes_accessed=2 * pairs * BLK * BLK + 16 * tiles * BLK * DH,
            transcendentals=0,
        ),
    )(pattern.reshape(-1), live_blocks, order, triple, triple, values, keys_t, probs)


def exchange(blocks):
    return lax.all_to_all(blocks, "ctx", split_axis=0, concat_axis=0, tiled=True)


def body(
    queries, keys, values, features, feat_grad, conv_weight, head_weight, pattern, live_blocks
):
    devices = lax.axis_size("ctx")
    frames, positions, channels = features.shape
    rows = frames * positions
    share = -(-conv_weight.size // devices // DH // 16) * 16

    incoming = lax.ppermute(feat_grad, "ctx", [(i + 1, i) for i in range(devices - 1)])
    triple, values = pack(queries, keys, values, share)
    triple, values, incoming = lax.optimization_barrier((triple, values, incoming))
    triple = decoder(feat_grad, incoming, features, conv_weight, head_weight, triple)

    triple = exchange(triple)
    values, triple, pattern, live_blocks = lax.optimization_barrier(
        (values, triple, pattern, live_blocks)
    )
    values = exchange(values)
    order = order_by_count(live_blocks)
    probs, keys_t, value_grad = probs_of(triple, rows, pattern, live_blocks, order, share)
    value_grad = share_sum(triple, value_grad, share)

    value_grad, values = lax.optimization_barrier((value_grad, values))
    value_grad = exchange(value_grad)
    grads = grads_of(triple, rows, values, keys_t, probs, pattern, live_blocks, order)
    grads, value_grad = lax.optimization_barrier((grads, value_grad))
    grads = exchange(grads)

    factor = 1.0 / math.sqrt(rows * devices)
    return tuple(unpack(grads, value_grad, conv_weight.shape, factor))


def solution(mesh):
    placed = (
        P(("clip", "ctx"), None),
        P(("clip", "ctx"), None),
        P(("clip", "ctx"), None),
        P(("clip", "ctx"), None, None),
        P(("clip", "ctx"), None, None),
        P(),
        P(),
        P("clip", None),
        P("clip"),
    )
    return jax.shard_map(
        body,
        mesh=mesh,
        in_specs=placed,
        out_specs=(
            P(("clip", "ctx"), None),
            P(("clip", "ctx"), None),
            P(("clip", "ctx"), None),
            P("clip", None, None),
        ),
        check_vma=False,
    )
```

```python
import functools
import math

import jax
import jax.numpy as jnp
from jax import lax
from jax.experimental import pallas as pl
from jax.experimental.pallas import tpu as pltpu
from jax.sharding import PartitionSpec as P

DH = 128
BLK = 128
TOGETHER = 4
PROBS_TOGETHER = 8
GROUP = 8
PACKED = 4
NT = (((1,), (1,)), ((), ()))
TN = (((0,), (0,)), ((), ()))
F32 = jnp.float32
BF16 = jnp.bfloat16
KERNEL_LIMIT = 56 * 1024 * 1024
SMALL_LIMIT = 16 * 1024 * 1024
MEDIUM_LIMIT = 32 * 1024 * 1024
HBM_SPEC = pl.BlockSpec(memory_space=pl.ANY)
VMEM_SPEC = pl.BlockSpec(memory_space=pltpu.VMEM)


def rows_of(tile):
    return tile >> 1, pl.ds(pl.multiple_of((tile & 1) * BLK, BLK), BLK)


def by_count(count, most, body):
    for size in range(1, most + 1):
        pl.when(count == size)(functools.partial(body, size))


def order_by_count(live_blocks):
    tiles = live_blocks.shape[0]
    ids = jnp.arange(tiles, dtype=jnp.int32)
    here, there = live_blocks[:, None], live_blocks[None, :]
    ahead = (there > here) | ((there == here) & (ids[None, :] < ids[:, None]))
    rank = jnp.sum(ahead.astype(jnp.int32), axis=1)
    placed = (rank[None, :] == ids[:, None]).astype(jnp.int32)
    return jnp.sum(placed * ids[None, :], axis=1)


def in_hbm(array):
    return pltpu.with_memory_space_constraint(array, pltpu.HBM)


def columns_of(ref, head):
    return ref.at[:, pl.ds(head * DH, DH)]


def pack_kernel(query_ref, key_ref, value_ref, triple_ref, last_ref, held_ref, in_sems, out_sems):
    rows = query_ref.shape[0]
    arrivals = [
        pltpu.make_async_copy(ref, held_ref.at[place], in_sems.at[place])
        for place, ref in enumerate((query_ref, key_ref, value_ref))
    ]
    for copy in arrivals:
        copy.start()
    departures = []
    for place, arrival in enumerate(arrivals):
        arrival.wait()
        for head in range(triple_ref.shape[0]):
            source = held_ref.at[place, :, pl.ds(head * DH, DH)]
            if place < 2:
                target = triple_ref.at[head, pl.ds(place * rows, rows), :]
            else:
                target = last_ref.at[head]
            departures.append(pltpu.make_async_copy(source, target, out_sems.at[place, head]))
            departures[-1].start()
    for copy in departures:
        copy.wait()


def pack(queries, keys, values, held):
    rows, width = queries.shape
    heads = width // DH
    return pl.pallas_call(
        pack_kernel,
        in_specs=[HBM_SPEC] * 3,
        out_specs=[HBM_SPEC] * 2,
        out_shape=[
            pltpu.HBM((heads, 3 * rows + held, DH), BF16),
            pltpu.HBM((heads, rows, DH), BF16),
        ],
        scratch_shapes=[
            pltpu.VMEM((3, rows, width), BF16),
            pltpu.SemaphoreType.DMA((3,)),
            pltpu.SemaphoreType.DMA((3, heads)),
        ],
        compiler_params=pltpu.CompilerParams(vmem_limit_bytes=SMALL_LIMIT),
        cost_estimate=pl.CostEstimate(flops=0, bytes_accessed=12 * rows * width, transcendentals=0),
    )(in_hbm(queries), in_hbm(keys), in_hbm(values))


def decoder_kernel(
    near_ref,
    next_ref,
    feature_ref,
    tap_weight_ref,
    head_weight_ref,
    triple_in_ref,
    triple_ref,
    held_ref,
    taps_ref,
    grad_sems,
    tap_sems,
):
    heads, rows, _ = held_ref.shape
    frames, positions, channels = feature_ref.shape
    devices = triple_ref.shape[0]
    share = taps_ref.shape[0] // devices
    steps = [near_ref[f] for f in range(frames)] + [next_ref[f] for f in range(frames)]
    taps = tap_weight_ref.shape[0]
    windows = [jnp.concatenate(steps[k : k + frames], 0) for k in range(taps)]
    feature_grad = sum(
        lax.dot_general(windows[k], tap_weight_ref[k], NT, preferred_element_type=F32)
        for k in range(taps)
    ).astype(BF16)
    copies = []
    for first in range(0, heads, PACKED):
        projected = lax.dot_general(
            feature_grad,
            head_weight_ref[first * DH : (first + PACKED) * DH, :],
            NT,
            preferred_element_type=F32,
        ).astype(BF16)
        for head in range(PACKED):
            held_ref[first + head] = projected[:, head * DH : (head + 1) * DH]
        group = pl.ds(first, PACKED)
        copies.append(
            pltpu.make_async_copy(
                held_ref.at[group],
                triple_ref.at[group, pl.ds(2 * rows, rows), :],
                grad_sems.at[first // PACKED],
            )
        )
        copies[-1].start()
    features_t = jnp.concatenate([feature_ref[f] for f in range(frames)], 0).T
    row = 0
    for k in range(taps):
        terms = jnp.dot(features_t, windows[k], preferred_element_type=F32).astype(BF16)
        for first in range(0, channels, DH):
            taps_ref[row : row + channels, :] = terms[:, first : first + DH]
            row += channels
    taps_ref[row:, :] = jnp.zeros((taps_ref.shape[0] - row, DH), BF16)
    for device in range(devices):
        copies.append(
            pltpu.make_async_copy(
                taps_ref.at[pl.ds(device * share, share), :],
                triple_ref.at[device, pl.ds(3 * rows, share), :],
                tap_sems.at[device],
            )
        )
        copies[-1].start()
    for copy in copies:
        copy.wait()


def decoder(feat_grad, incoming, features, conv_weight, head_weight, triple):
    heads, rows = triple.shape[0], features.shape[0] * features.shape[1]
    share = triple.shape[1] - 3 * rows
    return pl.pallas_call(
        decoder_kernel,
        in_specs=[VMEM_SPEC] * 5 + [HBM_SPEC],
        out_specs=HBM_SPEC,
        out_shape=pltpu.HBM(triple.shape, triple.dtype),
        scratch_shapes=[
            pltpu.VMEM((heads, rows, DH), BF16),
            pltpu.VMEM((heads * share, DH), BF16),
            pltpu.SemaphoreType.DMA((heads // PACKED,)),
            pltpu.SemaphoreType.DMA((heads,)),
        ],
        input_output_aliases={5: 0},
        compiler_params=pltpu.CompilerParams(vmem_limit_bytes=MEDIUM_LIMIT),
        cost_estimate=pl.CostEstimate(
            flops=2 * heads * rows * DH * head_weight.shape[1],
            bytes_accessed=6 * heads * rows * DH,
            transcendentals=0,
        ),
    )(feat_grad, incoming, features, conv_weight, head_weight, in_hbm(triple))


def unpack_kernel(factor, pair_ref, last_ref, *refs):
    *out_refs, tap_out_ref, taps_ref, scaled_ref, out_sems, done_sem = refs
    heads, rows = pair_ref.shape[0], out_refs[0].shape[0]
    share = last_ref.shape[1] - rows
    departures = []
    for part, (ref, start) in enumerate([(pair_ref, 0), (pair_ref, rows), (last_ref, 0)]):
        for head in range(heads):
            source = ref.at[head, pl.ds(start, rows), :]
            departures.append(
                pltpu.make_async_copy(
                    source, columns_of(out_refs[part], head), out_sems.at[part, head]
                )
            )
            departures[-1].start()
    for head in range(heads):
        taps_ref[head * share : (head + 1) * share, :] = last_ref[head, rows:, :]
    taps, channels, width = scaled_ref.shape
    row = 0
    for k in range(taps):
        for first in range(0, width, DH):
            terms = taps_ref[row : row + channels, :].astype(F32) * factor
            scaled_ref[k, :, first : first + DH] = terms
            row += channels
    departures.append(pltpu.make_async_copy(scaled_ref, tap_out_ref, done_sem))
    departures[-1].start()
    for copy in departures:
        copy.wait()


def unpack(pair, last, tap_shape, factor):
    heads, rows = pair.shape[0], pair.shape[1] // 2
    return pl.pallas_call(
        functools.partial(unpack_kernel, factor),
        in_specs=[VMEM_SPEC] * 2,
        out_specs=[HBM_SPEC] * 4,
        out_shape=[jax.ShapeDtypeStruct((rows, heads * DH), last.dtype)] * 3
        + [jax.ShapeDtypeStruct(tap_shape, F32)],
        scratch_shapes=[
            pltpu.VMEM((heads * (last.shape[1] - rows), DH), last.dtype),
            pltpu.VMEM(tap_shape, F32),
            pltpu.SemaphoreType.DMA((3, heads)),
            pltpu.SemaphoreType.DMA(()),
        ],
        compiler_params=pltpu.CompilerParams(vmem_limit_bytes=SMALL_LIMIT),
        cost_estimate=pl.CostEstimate(
            flops=0, bytes_accessed=12 * rows * heads * DH, transcendentals=0
        ),
    )(pair, last)


def clear(total_ref):
    def step(block, carry):
        total_ref[block] = jnp.zeros(total_ref.shape[1:], F32)
        return carry

    lax.fori_loop(0, total_ref.shape[0], step, 0)


def gather(ref, blocks, base=0):
    return jnp.concatenate(
        [ref[b >> 1, pl.ds(pl.multiple_of((b & 1) * BLK + base, BLK), BLK), :] for b in blocks], 0
    )


def probs_kernel(
    listed,
    pattern,
    live,
    order,
    query_ref,
    key_ref,
    grad_ref,
    terms_ref,
    probs_ref,
    key_t_ref,
    out_ref,
    total_ref,
    held_ref,
    sem,
):
    scale = DH ** (-0.5) * math.log2(math.e)
    step, steps = pl.program_id(0), pl.num_programs(0)

    rows, held = query_ref.shape[1], held_ref.shape[1]
    arrival = pltpu.make_async_copy(
        terms_ref.at[:, pl.ds(terms_ref.shape[1] - held, held), :], held_ref, sem
    )

    @pl.when(step == 0)
    def _():
        arrival.start()
        clear(total_ref)

    def group_step(group, carry):
        slots = [group * PROBS_TOGETHER + t for t in range(PROBS_TOGETHER)]
        tiles = [order[step * GROUP + slot] for slot in slots]

        def body(size):
            held = []
            for slot, tile in zip(slots, tiles):
                query = query_ref[rows_of(tile)]
                blocks = [pattern[tile * listed + j] for j in range(size)]
                scores = lax.dot_general(
                    gather(key_ref, blocks), query, NT, preferred_element_type=F32
                )
                key_block = lax.broadcasted_iota(jnp.int32, scores.shape, 0) >> 7
                scores = jnp.where(key_block < live[tile], scores, -jnp.inf)
                top = jnp.max(scores, axis=0, keepdims=True)
                weights = jnp.exp2((scores - top) * scale)
                inverse = 1.0 / jnp.sum(weights, axis=0, keepdims=True)
                probs = (weights * inverse).astype(BF16)
                probs_ref[slot, : size * BLK, :] = probs
                terms = jnp.dot(probs, grad_ref[rows_of(tile)], preferred_element_type=F32)
                held.append((blocks, terms))
            for blocks, terms in held:
                for j, b in enumerate(blocks):
                    total_ref[b] += terms[j * BLK : (j + 1) * BLK, :]

        by_count(live[tiles[0]], listed, body)
        for slot in slots:
            key_t_ref[slot] = key_ref[rows_of(step * GROUP + slot)].T
        return carry

    lax.fori_loop(0, GROUP // PROBS_TOGETHER, group_step, 0)

    @pl.when(step == steps - 1)
    def _():
        def finish(block, carry):
            out_ref[rows_of(block)] = total_ref[block].astype(BF16)
            return carry

        lax.fori_loop(0, total_ref.shape[0], finish, 0)
        arrival.wait()
        share = jnp.sum(held_ref[...].astype(F32), axis=0).astype(BF16)
        out_ref[:, rows:, :] = jnp.broadcast_to(share[None], held_ref.shape)


def whole(shape, index=None):
    index = (0,) * len(shape) if index is None else index
    return pl.BlockSpec(shape, lambda i, *_: index, pipeline_mode=pl.Buffered(1))


def probs_of(triple, rows, pattern, live_blocks, order, spare):
    tiles, listed = pattern.shape
    pairs = tiles * listed
    devices = triple.shape[0]
    part = (devices, rows, DH)
    return pl.pallas_call(
        functools.partial(probs_kernel, listed),
        grid_spec=pltpu.PrefetchScalarGridSpec(
            num_scalar_prefetch=3,
            grid=(tiles // GROUP,),
            in_specs=[whole(part, (0, place, 0)) for place in range(3)] + [HBM_SPEC],
            out_specs=[
                pl.BlockSpec((GROUP, listed * BLK, BLK), lambda i, *_: (i, 0, 0)),
                pl.BlockSpec((GROUP, DH, BLK), lambda i, *_: (i, 0, 0)),
                whole((devices, rows + spare, DH)),
            ],
            scratch_shapes=[
                pltpu.VMEM((tiles, BLK, DH), F32),
                pltpu.VMEM((devices, spare, DH), BF16),
                pltpu.SemaphoreType.DMA(()),
            ],
        ),
        out_shape=[
            jax.ShapeDtypeStruct((tiles, listed * BLK, BLK), BF16),
            jax.ShapeDtypeStruct((tiles, DH, BLK), BF16),
            pltpu.HBM((devices, rows + spare, DH), BF16),
        ],
        compiler_params=pltpu.CompilerParams(vmem_limit_bytes=KERNEL_LIMIT),
        cost_estimate=pl.CostEstimate(
            flops=4 * pairs * BLK * BLK * DH,
            bytes_accessed=2 * pairs * BLK * BLK,
            transcendentals=pairs * BLK * BLK,
        ),
    )(pattern.reshape(-1), live_blocks, order, triple, triple, triple, triple)


def grads_kernel(
    listed, pattern, live, order, query_ref, grad_ref, value_ref, key_t_ref, probs_ref, out_ref, total_ref
):
    scale = DH ** (-0.5)
    step, steps = pl.program_id(0), pl.num_programs(0)
    rows = query_ref.shape[1]

    @pl.when(step == 0)
    def _():
        clear(total_ref)

    def group_step(group, carry):
        slots = [group * TOGETHER + t for t in range(TOGETHER)]
        members = [order[step * GROUP + slot] for slot in slots]

        def body(size):
            held = []
            for slot, tile in zip(slots, members):
                blocks = [pattern[tile * listed + j] for j in range(size)]
                dprobs = lax.dot_general(
                    gather(value_ref, blocks), grad_ref[rows_of(tile)], NT, preferred_element_type=F32
                )
                probs = probs_ref[slot, : size * BLK, :].astype(F32)
                delta = jnp.sum(probs * dprobs, axis=0, keepdims=True)
                dscores = (probs * (dprobs - delta)).astype(BF16)
                keys_t = jnp.concatenate([key_t_ref[b] for b in blocks], 1)
                query_grad = jnp.dot(keys_t, dscores, preferred_element_type=F32)
                out_ref[rows_of(tile)] = (query_grad * scale).T.astype(BF16)
                terms = jnp.dot(dscores, query_ref[rows_of(tile)], preferred_element_type=F32)
                held.append((blocks, terms))
            for blocks, terms in held:
                for j, b in enumerate(blocks):
                    total_ref[b] += terms[j * BLK : (j + 1) * BLK, :]

        by_count(live[members[0]], listed, body)
        return carry

    lax.fori_loop(0, GROUP // TOGETHER, group_step, 0)

    @pl.when(step == steps - 1)
    def _():
        def finish(block, carry):
            start = pl.multiple_of((block & 1) * BLK + rows, BLK)
            out_ref[block >> 1, pl.ds(start, BLK), :] = (total_ref[block] * scale).astype(BF16)
            return carry

        lax.fori_loop(0, total_ref.shape[0], finish, 0)


def grads_of(triple, rows, values, keys_t, probs, pattern, live_blocks, order):
    tiles, listed = pattern.shape
    pairs = tiles * listed
    devices = triple.shape[0]
    part = (devices, rows, DH)
    return pl.pallas_call(
        functools.partial(grads_kernel, listed),
        grid_spec=pltpu.PrefetchScalarGridSpec(
            num_scalar_prefetch=3,
            grid=(tiles // GROUP,),
            in_specs=[
                whole(part),
                whole(part, (0, 2, 0)),
                whole(part),
                whole(keys_t.shape),
                pl.BlockSpec((GROUP, listed * BLK, BLK), lambda i, *_: (i, 0, 0)),
            ],
            out_specs=whole((devices, 2 * rows, DH)),
            scratch_shapes=[pltpu.VMEM((tiles, BLK, DH), F32)],
        ),
        out_shape=jax.ShapeDtypeStruct((devices, 2 * rows, DH), BF16),
        compiler_params=pltpu.CompilerParams(vmem_limit_bytes=KERNEL_LIMIT),
        cost_estimate=pl.CostEstimate(
            flops=6 * pairs * BLK * BLK * DH,
            bytes_accessed=2 * pairs * BLK * BLK + 16 * tiles * BLK * DH,
            transcendentals=0,
        ),
    )(pattern.reshape(-1), live_blocks, order, triple, triple, values, keys_t, probs)


def exchange(blocks):
    return lax.all_to_all(blocks, "ctx", split_axis=0, concat_axis=0, tiled=True)


def body(
    queries, keys, values, features, feat_grad, conv_weight, head_weight, pattern, live_blocks
):
    devices = lax.axis_size("ctx")
    frames, positions, channels = features.shape
    rows = frames * positions
    share = -(-conv_weight.size // devices // DH // 16) * 16

    incoming = lax.ppermute(feat_grad, "ctx", [(i + 1, i) for i in range(devices - 1)])
    triple, values = pack(queries, keys, values, share)
    triple, values, incoming = lax.optimization_barrier((triple, values, incoming))
    triple = decoder(feat_grad, incoming, features, conv_weight, head_weight, triple)

    triple = exchange(triple)
    values, triple, pattern, live_blocks = lax.optimization_barrier(
        (values, triple, pattern, live_blocks)
    )
    values = exchange(values)
    order = order_by_count(live_blocks)
    probs, keys_t, value_grad = probs_of(triple, rows, pattern, live_blocks, order, share)

    value_grad, values = lax.optimization_barrier((value_grad, values))
    value_grad = exchange(value_grad)
    grads = grads_of(triple, rows, values, keys_t, probs, pattern, live_blocks, order)
    grads, value_grad = lax.optimization_barrier((grads, value_grad))
    grads = exchange(grads)

    factor = 1.0 / math.sqrt(rows * devices)
    return tuple(unpack(grads, value_grad, conv_weight.shape, factor))


def solution(mesh):
    placed = (
        P(("clip", "ctx"), None),
        P(("clip", "ctx"), None),
        P(("clip", "ctx"), None),
        P(("clip", "ctx"), None, None),
        P(("clip", "ctx"), None, None),
        P(),
        P(),
        P("clip", None),
        P("clip"),
    )
    return jax.shard_map(
        body,
        mesh=mesh,
        in_specs=placed,
        out_specs=(
            P(("clip", "ctx"), None),
            P(("clip", "ctx"), None),
            P(("clip", "ctx"), None),
            P("clip", None, None),
        ),
        check_vma=False,
    )
```

```python
import functools
import math

import jax
import jax.numpy as jnp
from jax import lax
from jax.experimental import pallas as pl
from jax.experimental.pallas import tpu as pltpu
from jax.sharding import PartitionSpec as P

DH = 128
BLK = 128
TOGETHER = 4
PROBS_TOGETHER = 8
GROUP = 8
PACKED = 4
NT = (((1,), (1,)), ((), ()))
TN = (((0,), (0,)), ((), ()))
F32 = jnp.float32
BF16 = jnp.bfloat16
KERNEL_LIMIT = 56 * 1024 * 1024
SMALL_LIMIT = 16 * 1024 * 1024
MEDIUM_LIMIT = 32 * 1024 * 1024
HBM_SPEC = pl.BlockSpec(memory_space=pl.ANY)
VMEM_SPEC = pl.BlockSpec(memory_space=pltpu.VMEM)


def rows_of(tile):
    return tile >> 1, pl.ds(pl.multiple_of((tile & 1) * BLK, BLK), BLK)


def by_count(count, most, body):
    for size in range(1, most + 1):
        pl.when(count == size)(functools.partial(body, size))


def order_by_count(live_blocks):
    tiles = live_blocks.shape[0]
    ids = jnp.arange(tiles, dtype=jnp.int32)
    here, there = live_blocks[:, None], live_blocks[None, :]
    ahead = (there > here) | ((there == here) & (ids[None, :] < ids[:, None]))
    rank = jnp.sum(ahead.astype(jnp.int32), axis=1)
    placed = (rank[None, :] == ids[:, None]).astype(jnp.int32)
    return jnp.sum(placed * ids[None, :], axis=1)


def in_hbm(array):
    return pltpu.with_memory_space_constraint(array, pltpu.HBM)


def columns_of(ref, head):
    return ref.at[:, pl.ds(head * DH, DH)]


def pack_kernel(query_ref, key_ref, value_ref, triple_ref, last_ref, held_ref, in_sems, out_sems):
    rows = query_ref.shape[0]
    arrivals = [
        pltpu.make_async_copy(ref, held_ref.at[place], in_sems.at[place])
        for place, ref in enumerate((query_ref, key_ref, value_ref))
    ]
    for copy in arrivals:
        copy.start()
    departures = []
    for place, arrival in enumerate(arrivals):
        arrival.wait()
        for head in range(triple_ref.shape[0]):
            source = held_ref.at[place, :, pl.ds(head * DH, DH)]
            if place < 2:
                target = triple_ref.at[head, pl.ds(place * rows, rows), :]
            else:
                target = last_ref.at[head]
            departures.append(pltpu.make_async_copy(source, target, out_sems.at[place, head]))
            departures[-1].start()
    for copy in departures:
        copy.wait()


def pack(queries, keys, values, held):
    rows, width = queries.shape
    heads = width // DH
    return pl.pallas_call(
        pack_kernel,
        in_specs=[HBM_SPEC] * 3,
        out_specs=[HBM_SPEC] * 2,
        out_shape=[
            pltpu.HBM((heads, 3 * rows + held, DH), BF16),
            pltpu.HBM((heads, rows, DH), BF16),
        ],
        scratch_shapes=[
            pltpu.VMEM((3, rows, width), BF16),
            pltpu.SemaphoreType.DMA((3,)),
            pltpu.SemaphoreType.DMA((3, heads)),
        ],
        compiler_params=pltpu.CompilerParams(vmem_limit_bytes=SMALL_LIMIT),
        cost_estimate=pl.CostEstimate(flops=0, bytes_accessed=12 * rows * width, transcendentals=0),
    )(in_hbm(queries), in_hbm(keys), in_hbm(values))


def decoder_kernel(
    near_ref,
    next_ref,
    feature_ref,
    tap_weight_ref,
    head_weight_ref,
    triple_in_ref,
    triple_ref,
    held_ref,
    taps_ref,
    grad_sems,
    tap_sems,
):
    heads, rows, _ = held_ref.shape
    frames, positions, channels = feature_ref.shape
    devices = triple_ref.shape[0]
    share = taps_ref.shape[0] // devices
    steps = [near_ref[f] for f in range(frames)] + [next_ref[f] for f in range(frames)]
    taps = tap_weight_ref.shape[0]
    windows = [jnp.concatenate(steps[k : k + frames], 0) for k in range(taps)]
    feature_grad = sum(
        lax.dot_general(windows[k], tap_weight_ref[k], NT, preferred_element_type=F32)
        for k in range(taps)
    ).astype(BF16)
    copies = []
    for first in range(0, heads, PACKED):
        projected = lax.dot_general(
            feature_grad,
            head_weight_ref[first * DH : (first + PACKED) * DH, :],
            NT,
            preferred_element_type=F32,
        ).astype(BF16)
        for head in range(PACKED):
            held_ref[first + head] = projected[:, head * DH : (head + 1) * DH]
        group = pl.ds(first, PACKED)
        copies.append(
            pltpu.make_async_copy(
                held_ref.at[group],
                triple_ref.at[group, pl.ds(2 * rows, rows), :],
                grad_sems.at[first // PACKED],
            )
        )
        copies[-1].start()
    features_t = jnp.concatenate([feature_ref[f] for f in range(frames)], 0).T
    row = 0
    for k in range(taps):
        terms = jnp.dot(features_t, windows[k], preferred_element_type=F32).astype(BF16)
        for first in range(0, channels, DH):
            taps_ref[row : row + channels, :] = terms[:, first : first + DH]
            row += channels
    taps_ref[row:, :] = jnp.zeros((taps_ref.shape[0] - row, DH), BF16)
    for device in range(devices):
        copies.append(
            pltpu.make_async_copy(
                taps_ref.at[pl.ds(device * share, share), :],
                triple_ref.at[device, pl.ds(3 * rows, share), :],
                tap_sems.at[device],
            )
        )
        copies[-1].start()
    for copy in copies:
        copy.wait()


def decoder(feat_grad, incoming, features, conv_weight, head_weight, triple):
    heads, rows = triple.shape[0], features.shape[0] * features.shape[1]
    share = triple.shape[1] - 3 * rows
    return pl.pallas_call(
        decoder_kernel,
        in_specs=[VMEM_SPEC] * 5 + [HBM_SPEC],
        out_specs=HBM_SPEC,
        out_shape=pltpu.HBM(triple.shape, triple.dtype),
        scratch_shapes=[
            pltpu.VMEM((heads, rows, DH), BF16),
            pltpu.VMEM((heads * share, DH), BF16),
            pltpu.SemaphoreType.DMA((heads // PACKED,)),
            pltpu.SemaphoreType.DMA((heads,)),
        ],
        input_output_aliases={5: 0},
        compiler_params=pltpu.CompilerParams(vmem_limit_bytes=MEDIUM_LIMIT),
        cost_estimate=pl.CostEstimate(
            flops=2 * heads * rows * DH * head_weight.shape[1],
            bytes_accessed=6 * heads * rows * DH,
            transcendentals=0,
        ),
    )(feat_grad, incoming, features, conv_weight, head_weight, in_hbm(triple))


def unpack_kernel(factor, pair_ref, last_ref, *refs):
    *out_refs, tap_out_ref, taps_ref, scaled_ref, out_sems, done_sem = refs
    heads, rows = pair_ref.shape[0], out_refs[0].shape[0]
    share = last_ref.shape[1] - rows
    departures = []
    for part, (ref, start) in enumerate([(pair_ref, 0), (pair_ref, rows), (last_ref, 0)]):
        for head in range(heads):
            source = ref.at[head, pl.ds(start, rows), :]
            departures.append(
                pltpu.make_async_copy(
                    source, columns_of(out_refs[part], head), out_sems.at[part, head]
                )
            )
            departures[-1].start()
    for head in range(heads):
        taps_ref[head * share : (head + 1) * share, :] = last_ref[head, rows:, :]
    taps, channels, width = scaled_ref.shape
    row = 0
    for k in range(taps):
        for first in range(0, width, DH):
            terms = taps_ref[row : row + channels, :].astype(F32) * factor
            scaled_ref[k, :, first : first + DH] = terms
            row += channels
    departures.append(pltpu.make_async_copy(scaled_ref, tap_out_ref, done_sem))
    departures[-1].start()
    for copy in departures:
        copy.wait()


def unpack(pair, last, tap_shape, factor):
    heads, rows = pair.shape[0], pair.shape[1] // 2
    return pl.pallas_call(
        functools.partial(unpack_kernel, factor),
        in_specs=[VMEM_SPEC] * 2,
        out_specs=[HBM_SPEC] * 4,
        out_shape=[jax.ShapeDtypeStruct((rows, heads * DH), last.dtype)] * 3
        + [jax.ShapeDtypeStruct(tap_shape, F32)],
        scratch_shapes=[
            pltpu.VMEM((heads * (last.shape[1] - rows), DH), last.dtype),
            pltpu.VMEM(tap_shape, F32),
            pltpu.SemaphoreType.DMA((3, heads)),
            pltpu.SemaphoreType.DMA(()),
        ],
        compiler_params=pltpu.CompilerParams(vmem_limit_bytes=SMALL_LIMIT),
        cost_estimate=pl.CostEstimate(
            flops=0, bytes_accessed=12 * rows * heads * DH, transcendentals=0
        ),
    )(pair, last)


def clear(total_ref):
    def step(block, carry):
        total_ref[block] = jnp.zeros(total_ref.shape[1:], F32)
        return carry

    lax.fori_loop(0, total_ref.shape[0], step, 0)


def gather(ref, blocks, base=0):
    return jnp.concatenate(
        [ref[b >> 1, pl.ds(pl.multiple_of((b & 1) * BLK + base, BLK), BLK), :] for b in blocks], 0
    )


def probs_kernel(
    listed,
    pattern,
    live,
    order,
    query_ref,
    key_ref,
    grad_ref,
    terms_ref,
    probs_ref,
    out_ref,
    total_ref,
    held_ref,
    sem,
):
    scale = DH ** (-0.5) * math.log2(math.e)
    step, steps = pl.program_id(0), pl.num_programs(0)

    rows, held = query_ref.shape[1], held_ref.shape[1]
    arrival = pltpu.make_async_copy(
        terms_ref.at[:, pl.ds(terms_ref.shape[1] - held, held), :], held_ref, sem
    )

    @pl.when(step == 0)
    def _():
        arrival.start()
        clear(total_ref)

    def group_step(group, carry):
        slots = [group * PROBS_TOGETHER + t for t in range(PROBS_TOGETHER)]
        tiles = [order[step * GROUP + slot] for slot in slots]

        def body(size):
            held = []
            for slot, tile in zip(slots, tiles):
                query = query_ref[rows_of(tile)]
                blocks = [pattern[tile * listed + j] for j in range(size)]
                scores = lax.dot_general(
                    gather(key_ref, blocks), query, NT, preferred_element_type=F32
                )
                key_block = lax.broadcasted_iota(jnp.int32, scores.shape, 0) >> 7
                scores = jnp.where(key_block < live[tile], scores, -jnp.inf)
                top = jnp.max(scores, axis=0, keepdims=True)
                weights = jnp.exp2((scores - top) * scale)
                inverse = 1.0 / jnp.sum(weights, axis=0, keepdims=True)
                probs = (weights * inverse).astype(BF16)
                probs_ref[slot, : size * BLK, :] = probs
                terms = jnp.dot(probs, grad_ref[rows_of(tile)], preferred_element_type=F32)
                held.append((blocks, terms))
            for blocks, terms in held:
                for j, b in enumerate(blocks):
                    total_ref[b] += terms[j * BLK : (j + 1) * BLK, :]

        by_count(live[tiles[0]], listed, body)
        return carry

    lax.fori_loop(0, GROUP // PROBS_TOGETHER, group_step, 0)

    @pl.when(step == steps - 1)
    def _():
        def finish(block, carry):
            out_ref[rows_of(block)] = total_ref[block].astype(BF16)
            return carry

        lax.fori_loop(0, total_ref.shape[0], finish, 0)
        arrival.wait()
        share = jnp.sum(held_ref[...].astype(F32), axis=0).astype(BF16)
        out_ref[:, rows:, :] = jnp.broadcast_to(share[None], held_ref.shape)


def whole(shape, index=None):
    index = (0,) * len(shape) if index is None else index
    return pl.BlockSpec(shape, lambda i, *_: index, pipeline_mode=pl.Buffered(1))


def probs_of(triple, rows, pattern, live_blocks, order, spare):
    tiles, listed = pattern.shape
    pairs = tiles * listed
    devices = triple.shape[0]
    part = (devices, rows, DH)
    return pl.pallas_call(
        functools.partial(probs_kernel, listed),
        grid_spec=pltpu.PrefetchScalarGridSpec(
            num_scalar_prefetch=3,
            grid=(tiles // GROUP,),
            in_specs=[whole(part, (0, place, 0)) for place in range(3)] + [HBM_SPEC],
            out_specs=[
                pl.BlockSpec((GROUP, listed * BLK, BLK), lambda i, *_: (i, 0, 0)),
                whole((devices, rows + spare, DH)),
            ],
            scratch_shapes=[
                pltpu.VMEM((tiles, BLK, DH), F32),
                pltpu.VMEM((devices, spare, DH), BF16),
                pltpu.SemaphoreType.DMA(()),
            ],
        ),
        out_shape=[
            jax.ShapeDtypeStruct((tiles, listed * BLK, BLK), BF16),
            pltpu.HBM((devices, rows + spare, DH), BF16),
        ],
        compiler_params=pltpu.CompilerParams(vmem_limit_bytes=KERNEL_LIMIT),
        cost_estimate=pl.CostEstimate(
            flops=4 * pairs * BLK * BLK * DH,
            bytes_accessed=2 * pairs * BLK * BLK,
            transcendentals=pairs * BLK * BLK,
        ),
    )(pattern.reshape(-1), live_blocks, order, triple, triple, triple, triple)


def grads_kernel(
    listed, pattern, live, order, query_ref, grad_ref, value_ref, key_ref, probs_ref, out_ref, total_ref, key_t_ref
):
    scale = DH ** (-0.5)
    step, steps = pl.program_id(0), pl.num_programs(0)
    rows = query_ref.shape[1]

    @pl.when(step == 0)
    def _():
        clear(total_ref)

        def transpose(group, carry):
            for t in range(GROUP):
                block = group * GROUP + t
                key_t_ref[block] = key_ref[rows_of(block)].T
            return carry

        lax.fori_loop(0, key_t_ref.shape[0] // GROUP, transpose, 0)

    def group_step(group, carry):
        slots = [group * TOGETHER + t for t in range(TOGETHER)]
        members = [order[step * GROUP + slot] for slot in slots]

        def body(size):
            held = []
            for slot, tile in zip(slots, members):
                blocks = [pattern[tile * listed + j] for j in range(size)]
                dprobs = lax.dot_general(
                    gather(value_ref, blocks), grad_ref[rows_of(tile)], NT, preferred_element_type=F32
                )
                probs = probs_ref[slot, : size * BLK, :].astype(F32)
                delta = jnp.sum(probs * dprobs, axis=0, keepdims=True)
                dscores = (probs * (dprobs - delta)).astype(BF16)
                keys_t = jnp.concatenate([key_t_ref[b] for b in blocks], 1)
                query_grad = jnp.dot(keys_t, dscores, preferred_element_type=F32)
                out_ref[rows_of(tile)] = (query_grad * scale).T.astype(BF16)
                terms = jnp.dot(dscores, query_ref[rows_of(tile)], preferred_element_type=F32)
                held.append((blocks, terms))
            for blocks, terms in held:
                for j, b in enumerate(blocks):
                    total_ref[b] += terms[j * BLK : (j + 1) * BLK, :]

        by_count(live[members[0]], listed, body)
        return carry

    lax.fori_loop(0, GROUP // TOGETHER, group_step, 0)

    @pl.when(step == steps - 1)
    def _():
        def finish(block, carry):
            start = pl.multiple_of((block & 1) * BLK + rows, BLK)
            out_ref[block >> 1, pl.ds(start, BLK), :] = (total_ref[block] * scale).astype(BF16)
            return carry

        lax.fori_loop(0, total_ref.shape[0], finish, 0)


def grads_of(triple, rows, values, probs, pattern, live_blocks, order):
    tiles, listed = pattern.shape
    pairs = tiles * listed
    devices = triple.shape[0]
    part = (devices, rows, DH)
    return pl.pallas_call(
        functools.partial(grads_kernel, listed),
        grid_spec=pltpu.PrefetchScalarGridSpec(
            num_scalar_prefetch=3,
            grid=(tiles // GROUP,),
            in_specs=[
                whole(part),
                whole(part, (0, 2, 0)),
                whole(part),
                whole(part, (0, 1, 0)),
                pl.BlockSpec((GROUP, listed * BLK, BLK), lambda i, *_: (i, 0, 0)),
            ],
            out_specs=whole((devices, 2 * rows, DH)),
            scratch_shapes=[
                pltpu.VMEM((tiles, BLK, DH), F32),
                pltpu.VMEM((tiles, DH, BLK), BF16),
            ],
        ),
        out_shape=jax.ShapeDtypeStruct((devices, 2 * rows, DH), BF16),
        compiler_params=pltpu.CompilerParams(vmem_limit_bytes=KERNEL_LIMIT),
        cost_estimate=pl.CostEstimate(
            flops=6 * pairs * BLK * BLK * DH,
            bytes_accessed=2 * pairs * BLK * BLK + 16 * tiles * BLK * DH,
            transcendentals=0,
        ),
    )(pattern.reshape(-1), live_blocks, order, triple, triple, values, triple, probs)


def exchange(blocks):
    return lax.all_to_all(blocks, "ctx", split_axis=0, concat_axis=0, tiled=True)


def body(
    queries, keys, values, features, feat_grad, conv_weight, head_weight, pattern, live_blocks
):
    devices = lax.axis_size("ctx")
    frames, positions, channels = features.shape
    rows = frames * positions
    share = -(-conv_weight.size // devices // DH // 16) * 16

    incoming = lax.ppermute(feat_grad, "ctx", [(i + 1, i) for i in range(devices - 1)])
    triple, values = pack(queries, keys, values, share)
    triple, values, incoming = lax.optimization_barrier((triple, values, incoming))
    triple = decoder(feat_grad, incoming, features, conv_weight, head_weight, triple)

    triple = exchange(triple)
    values, triple, pattern, live_blocks = lax.optimization_barrier(
        (values, triple, pattern, live_blocks)
    )
    values = exchange(values)
    order = order_by_count(live_blocks)
    probs, value_grad = probs_of(triple, rows, pattern, live_blocks, order, share)

    value_grad, values = lax.optimization_barrier((value_grad, values))
    value_grad = exchange(value_grad)
    grads = grads_of(triple, rows, values, probs, pattern, live_blocks, order)
    grads, value_grad = lax.optimization_barrier((grads, value_grad))
    grads = exchange(grads)

    factor = 1.0 / math.sqrt(rows * devices)
    return tuple(unpack(grads, value_grad, conv_weight.shape, factor))


def solution(mesh):
    placed = (
        P(("clip", "ctx"), None),
        P(("clip", "ctx"), None),
        P(("clip", "ctx"), None),
        P(("clip", "ctx"), None, None),
        P(("clip", "ctx"), None, None),
        P(),
        P(),
        P("clip", None),
        P("clip"),
    )
    return jax.shard_map(
        body,
        mesh=mesh,
        in_specs=placed,
        out_specs=(
            P(("clip", "ctx"), None),
            P(("clip", "ctx"), None),
            P(("clip", "ctx"), None),
            P("clip", None, None),
        ),
        check_vma=False,
    )
```

```python
import functools
import math

import jax
import jax.numpy as jnp
from jax import lax
from jax.experimental import pallas as pl
from jax.experimental.pallas import tpu as pltpu
from jax.sharding import PartitionSpec as P

DH = 128
BLK = 128
TOGETHER = 4
PROBS_TOGETHER = 8
GROUP = 8
PACKED = 4
NT = (((1,), (1,)), ((), ()))
TN = (((0,), (0,)), ((), ()))
F32 = jnp.float32
BF16 = jnp.bfloat16
KERNEL_LIMIT = 56 * 1024 * 1024
SMALL_LIMIT = 16 * 1024 * 1024
MEDIUM_LIMIT = 32 * 1024 * 1024
HBM_SPEC = pl.BlockSpec(memory_space=pl.ANY)
VMEM_SPEC = pl.BlockSpec(memory_space=pltpu.VMEM)


def rows_of(tile):
    return tile >> 1, pl.ds(pl.multiple_of((tile & 1) * BLK, BLK), BLK)


def by_count(count, most, body):
    for size in range(1, most + 1):
        pl.when(count == size)(functools.partial(body, size))


def order_by_count(live_blocks):
    tiles = live_blocks.shape[0]
    ids = jnp.arange(tiles, dtype=jnp.int32)
    here, there = live_blocks[:, None], live_blocks[None, :]
    ahead = (there > here) | ((there == here) & (ids[None, :] < ids[:, None]))
    rank = jnp.sum(ahead.astype(jnp.int32), axis=1)
    placed = (rank[None, :] == ids[:, None]).astype(jnp.int32)
    return jnp.sum(placed * ids[None, :], axis=1)


def in_hbm(array):
    return pltpu.with_memory_space_constraint(array, pltpu.HBM)


def columns_of(ref, head):
    return ref.at[:, pl.ds(head * DH, DH)]


def pack_kernel(query_ref, key_ref, value_ref, triple_ref, last_ref, held_ref, in_sems, out_sems):
    rows = query_ref.shape[0]
    arrivals = [
        pltpu.make_async_copy(ref, held_ref.at[place], in_sems.at[place])
        for place, ref in enumerate((query_ref, key_ref, value_ref))
    ]
    for copy in arrivals:
        copy.start()
    departures = []
    for place, arrival in enumerate(arrivals):
        arrival.wait()
        for head in range(triple_ref.shape[0]):
            source = held_ref.at[place, :, pl.ds(head * DH, DH)]
            if place < 2:
                target = triple_ref.at[head, pl.ds(place * rows, rows), :]
            else:
                target = last_ref.at[head]
            departures.append(pltpu.make_async_copy(source, target, out_sems.at[place, head]))
            departures[-1].start()
    for copy in departures:
        copy.wait()


def pack(queries, keys, values, held):
    rows, width = queries.shape
    heads = width // DH
    return pl.pallas_call(
        pack_kernel,
        in_specs=[HBM_SPEC] * 3,
        out_specs=[HBM_SPEC] * 2,
        out_shape=[
            pltpu.HBM((heads, 3 * rows + held, DH), BF16),
            pltpu.HBM((heads, rows, DH), BF16),
        ],
        scratch_shapes=[
            pltpu.VMEM((3, rows, width), BF16),
            pltpu.SemaphoreType.DMA((3,)),
            pltpu.SemaphoreType.DMA((3, heads)),
        ],
        compiler_params=pltpu.CompilerParams(vmem_limit_bytes=SMALL_LIMIT),
        cost_estimate=pl.CostEstimate(flops=0, bytes_accessed=12 * rows * width, transcendentals=0),
    )(in_hbm(queries), in_hbm(keys), in_hbm(values))


def decoder_kernel(
    near_ref,
    next_ref,
    feature_ref,
    tap_weight_ref,
    head_weight_ref,
    triple_in_ref,
    triple_ref,
    held_ref,
    taps_ref,
    grad_sems,
    tap_sems,
):
    heads, rows, _ = held_ref.shape
    frames, positions, channels = feature_ref.shape
    devices = triple_ref.shape[0]
    share = taps_ref.shape[0] // devices
    steps = [near_ref[f] for f in range(frames)] + [next_ref[f] for f in range(frames)]
    taps = tap_weight_ref.shape[0]
    windows = [jnp.concatenate(steps[k : k + frames], 0) for k in range(taps)]
    feature_grad = sum(
        lax.dot_general(windows[k], tap_weight_ref[k], NT, preferred_element_type=F32)
        for k in range(taps)
    ).astype(BF16)
    copies = []
    for first in range(0, heads, PACKED):
        projected = lax.dot_general(
            feature_grad,
            head_weight_ref[first * DH : (first + PACKED) * DH, :],
            NT,
            preferred_element_type=F32,
        ).astype(BF16)
        for head in range(PACKED):
            held_ref[first + head] = projected[:, head * DH : (head + 1) * DH]
        group = pl.ds(first, PACKED)
        copies.append(
            pltpu.make_async_copy(
                held_ref.at[group],
                triple_ref.at[group, pl.ds(2 * rows, rows), :],
                grad_sems.at[first // PACKED],
            )
        )
        copies[-1].start()
    features_t = jnp.concatenate([feature_ref[f] for f in range(frames)], 0).T
    row = 0
    for k in range(taps):
        terms = jnp.dot(features_t, windows[k], preferred_element_type=F32).astype(BF16)
        for first in range(0, channels, DH):
            taps_ref[row : row + channels, :] = terms[:, first : first + DH]
            row += channels
    taps_ref[row:, :] = jnp.zeros((taps_ref.shape[0] - row, DH), BF16)
    for device in range(devices):
        copies.append(
            pltpu.make_async_copy(
                taps_ref.at[pl.ds(device * share, share), :],
                triple_ref.at[device, pl.ds(3 * rows, share), :],
                tap_sems.at[device],
            )
        )
        copies[-1].start()
    for copy in copies:
        copy.wait()


def decoder(feat_grad, incoming, features, conv_weight, head_weight, triple):
    heads, rows = triple.shape[0], features.shape[0] * features.shape[1]
    share = triple.shape[1] - 3 * rows
    return pl.pallas_call(
        decoder_kernel,
        in_specs=[VMEM_SPEC] * 5 + [HBM_SPEC],
        out_specs=HBM_SPEC,
        out_shape=pltpu.HBM(triple.shape, triple.dtype),
        scratch_shapes=[
            pltpu.VMEM((heads, rows, DH), BF16),
            pltpu.VMEM((heads * share, DH), BF16),
            pltpu.SemaphoreType.DMA((heads // PACKED,)),
            pltpu.SemaphoreType.DMA((heads,)),
        ],
        input_output_aliases={5: 0},
        compiler_params=pltpu.CompilerParams(vmem_limit_bytes=MEDIUM_LIMIT),
        cost_estimate=pl.CostEstimate(
            flops=2 * heads * rows * DH * head_weight.shape[1],
            bytes_accessed=6 * heads * rows * DH,
            transcendentals=0,
        ),
    )(feat_grad, incoming, features, conv_weight, head_weight, in_hbm(triple))


def unpack_kernel(factor, pair_ref, last_ref, *refs):
    *out_refs, tap_out_ref, taps_ref, scaled_ref, out_sems, done_sem = refs
    heads, rows = pair_ref.shape[0], out_refs[0].shape[0]
    share = last_ref.shape[1] - rows
    departures = []
    for part, (ref, start) in enumerate([(pair_ref, 0), (pair_ref, rows), (last_ref, 0)]):
        for head in range(heads):
            source = ref.at[head, pl.ds(start, rows), :]
            departures.append(
                pltpu.make_async_copy(
                    source, columns_of(out_refs[part], head), out_sems.at[part, head]
                )
            )
            departures[-1].start()
    for head in range(heads):
        taps_ref[head * share : (head + 1) * share, :] = last_ref[head, rows:, :]
    taps, channels, width = scaled_ref.shape
    row = 0
    for k in range(taps):
        for first in range(0, width, DH):
            terms = taps_ref[row : row + channels, :].astype(F32) * factor
            scaled_ref[k, :, first : first + DH] = terms
            row += channels
    departures.append(pltpu.make_async_copy(scaled_ref, tap_out_ref, done_sem))
    departures[-1].start()
    for copy in departures:
        copy.wait()


def unpack(pair, last, tap_shape, factor):
    heads, rows = pair.shape[0], pair.shape[1] // 2
    return pl.pallas_call(
        functools.partial(unpack_kernel, factor),
        in_specs=[VMEM_SPEC] * 2,
        out_specs=[HBM_SPEC] * 4,
        out_shape=[jax.ShapeDtypeStruct((rows, heads * DH), last.dtype)] * 3
        + [jax.ShapeDtypeStruct(tap_shape, F32)],
        scratch_shapes=[
            pltpu.VMEM((heads * (last.shape[1] - rows), DH), last.dtype),
            pltpu.VMEM(tap_shape, F32),
            pltpu.SemaphoreType.DMA((3, heads)),
            pltpu.SemaphoreType.DMA(()),
        ],
        compiler_params=pltpu.CompilerParams(vmem_limit_bytes=SMALL_LIMIT),
        cost_estimate=pl.CostEstimate(
            flops=0, bytes_accessed=12 * rows * heads * DH, transcendentals=0
        ),
    )(pair, last)


def clear(total_ref):
    def step(block, carry):
        total_ref[block] = jnp.zeros(total_ref.shape[1:], F32)
        return carry

    lax.fori_loop(0, total_ref.shape[0], step, 0)


def gather(ref, blocks, base=0):
    return jnp.concatenate(
        [ref[b >> 1, pl.ds(pl.multiple_of((b & 1) * BLK + base, BLK), BLK), :] for b in blocks], 0
    )


def probs_kernel(
    listed,
    pattern,
    live,
    order,
    query_ref,
    key_ref,
    grad_ref,
    terms_ref,
    probs_ref,
    out_ref,
    total_ref,
    held_ref,
    sem,
):
    scale = DH ** (-0.5) * math.log2(math.e)
    step, steps = pl.program_id(0), pl.num_programs(0)

    rows, held = query_ref.shape[1], held_ref.shape[1]
    arrival = pltpu.make_async_copy(
        terms_ref.at[:, pl.ds(terms_ref.shape[1] - held, held), :], held_ref, sem
    )

    @pl.when(step == 0)
    def _():
        arrival.start()
        clear(total_ref)

    def group_step(group, carry):
        slots = [group * PROBS_TOGETHER + t for t in range(PROBS_TOGETHER)]
        tiles = [order[step * GROUP + slot] for slot in slots]

        def body(size):
            held = []
            for slot, tile in zip(slots, tiles):
                query = query_ref[rows_of(tile)]
                blocks = [pattern[tile * listed + j] for j in range(size)]
                scores = lax.dot_general(
                    gather(key_ref, blocks), query, NT, preferred_element_type=F32
                )
                key_block = lax.broadcasted_iota(jnp.int32, scores.shape, 0) >> 7
                scores = jnp.where(key_block < live[tile], scores, -jnp.inf)
                top = jnp.max(scores, axis=0, keepdims=True)
                weights = jnp.exp2((scores - top) * scale)
                inverse = 1.0 / jnp.sum(weights, axis=0, keepdims=True)
                probs = (weights * inverse).astype(BF16)
                probs_ref[slot, : size * BLK, :] = probs
                terms = jnp.dot(probs, grad_ref[rows_of(tile)], preferred_element_type=F32)
                held.append((blocks, terms))
            for blocks, terms in held:
                for j, b in enumerate(blocks):
                    total_ref[b] += terms[j * BLK : (j + 1) * BLK, :]

        by_count(live[tiles[0]], listed, body)
        return carry

    lax.fori_loop(0, GROUP // PROBS_TOGETHER, group_step, 0)

    @pl.when(step == steps - 1)
    def _():
        def finish(block, carry):
            out_ref[rows_of(block)] = total_ref[block].astype(BF16)
            return carry

        lax.fori_loop(0, total_ref.shape[0], finish, 0)
        arrival.wait()
        share = jnp.sum(held_ref[...].astype(F32), axis=0).astype(BF16)
        out_ref[:, rows:, :] = jnp.broadcast_to(share[None], held_ref.shape)


def whole(shape, index=None):
    index = (0,) * len(shape) if index is None else index
    return pl.BlockSpec(shape, lambda i, *_: index, pipeline_mode=pl.Buffered(1))


def probs_of(triple, rows, pattern, live_blocks, order, spare):
    tiles, listed = pattern.shape
    pairs = tiles * listed
    devices = triple.shape[0]
    part = (devices, rows, DH)
    return pl.pallas_call(
        functools.partial(probs_kernel, listed),
        grid_spec=pltpu.PrefetchScalarGridSpec(
            num_scalar_prefetch=3,
            grid=(tiles // GROUP,),
            in_specs=[whole(part, (0, place, 0)) for place in range(3)] + [HBM_SPEC],
            out_specs=[
                pl.BlockSpec((GROUP, listed * BLK, BLK), lambda i, *_: (i, 0, 0)),
                whole((devices, rows + spare, DH)),
            ],
            scratch_shapes=[
                pltpu.VMEM((tiles, BLK, DH), F32),
                pltpu.VMEM((devices, spare, DH), BF16),
                pltpu.SemaphoreType.DMA(()),
            ],
        ),
        out_shape=[
            jax.ShapeDtypeStruct((tiles, listed * BLK, BLK), BF16),
            pltpu.HBM((devices, rows + spare, DH), BF16),
        ],
        compiler_params=pltpu.CompilerParams(vmem_limit_bytes=KERNEL_LIMIT),
        cost_estimate=pl.CostEstimate(
            flops=4 * pairs * BLK * BLK * DH,
            bytes_accessed=2 * pairs * BLK * BLK,
            transcendentals=pairs * BLK * BLK,
        ),
    )(pattern.reshape(-1), live_blocks, order, triple, triple, triple, triple)


def grads_kernel(
    listed, pattern, live, order, query_ref, grad_ref, value_ref, key_ref, probs_ref, out_ref, total_ref, key_t_ref
):
    scale = DH ** (-0.5)
    step, steps = pl.program_id(0), pl.num_programs(0)
    rows = query_ref.shape[1]

    @pl.when(step == 0)
    def _():
        clear(total_ref)

        def transpose(group, carry):
            for t in range(GROUP):
                block = group * GROUP + t
                key_t_ref[block] = key_ref[rows_of(block)].T
            return carry

        lax.fori_loop(0, key_t_ref.shape[0] // GROUP, transpose, 0)

    def group_step(group, carry):
        slots = [group * TOGETHER + t for t in range(TOGETHER)]
        members = [order[step * GROUP + slot] for slot in slots]

        def body(size):
            held = []
            for slot, tile in zip(slots, members):
                blocks = [pattern[tile * listed + j] for j in range(size)]
                dprobs = lax.dot_general(
                    gather(value_ref, blocks), grad_ref[rows_of(tile)], NT, preferred_element_type=F32
                )
                probs = probs_ref[slot, : size * BLK, :].astype(F32)
                delta = jnp.sum(probs * dprobs, axis=0, keepdims=True)
                dscores = (probs * (dprobs - delta)).astype(BF16)
                keys_t = jnp.concatenate([key_t_ref[b] for b in blocks], 1)
                query_grad = jnp.dot(keys_t, dscores, preferred_element_type=F32)
                out_ref[rows_of(tile)] = (query_grad * scale).T.astype(BF16)
                terms = jnp.dot(dscores, query_ref[rows_of(tile)], preferred_element_type=F32)
                held.append((blocks, terms))
            for blocks, terms in held:
                for j, b in enumerate(blocks):
                    total_ref[b] += terms[j * BLK : (j + 1) * BLK, :]

        by_count(live[members[0]], listed, body)
        return carry

    lax.fori_loop(0, GROUP // TOGETHER, group_step, 0)

    @pl.when(step == steps - 1)
    def _():
        def finish(block, carry):
            start = pl.multiple_of((block & 1) * BLK + rows, BLK)
            out_ref[block >> 1, pl.ds(start, BLK), :] = (total_ref[block] * scale).astype(BF16)
            return carry

        lax.fori_loop(0, total_ref.shape[0], finish, 0)


def grads_of(triple, rows, values, probs, pattern, live_blocks, order):
    tiles, listed = pattern.shape
    pairs = tiles * listed
    devices = triple.shape[0]
    part = (devices, rows, DH)
    return pl.pallas_call(
        functools.partial(grads_kernel, listed),
        grid_spec=pltpu.PrefetchScalarGridSpec(
            num_scalar_prefetch=3,
            grid=(tiles // GROUP,),
            in_specs=[
                whole(part),
                whole(part, (0, 2, 0)),
                whole(part),
                whole(part, (0, 1, 0)),
                pl.BlockSpec((GROUP, listed * BLK, BLK), lambda i, *_: (i, 0, 0)),
            ],
            out_specs=whole((devices, 2 * rows, DH)),
            scratch_shapes=[
                pltpu.VMEM((tiles, BLK, DH), F32),
                pltpu.VMEM((tiles, DH, BLK), BF16),
            ],
        ),
        out_shape=jax.ShapeDtypeStruct((devices, 2 * rows, DH), BF16),
        compiler_params=pltpu.CompilerParams(vmem_limit_bytes=KERNEL_LIMIT),
        cost_estimate=pl.CostEstimate(
            flops=6 * pairs * BLK * BLK * DH,
            bytes_accessed=2 * pairs * BLK * BLK + 16 * tiles * BLK * DH,
            transcendentals=0,
        ),
    )(pattern.reshape(-1), live_blocks, order, triple, triple, values, triple, probs)


def exchange(blocks):
    return lax.all_to_all(blocks, "ctx", split_axis=0, concat_axis=0, tiled=True)


def body(
    queries, keys, values, features, feat_grad, conv_weight, head_weight, pattern, live_blocks
):
    devices = lax.axis_size("ctx")
    frames, positions, channels = features.shape
    rows = frames * positions
    share = -(-conv_weight.size // devices // DH // 16) * 16

    incoming = lax.ppermute(feat_grad, "ctx", [(i + 1, i) for i in range(devices - 1)])
    triple, values = pack(queries, keys, values, share)
    order = order_by_count(live_blocks)
    triple, values, incoming, order = lax.optimization_barrier((triple, values, incoming, order))
    triple = decoder(feat_grad, incoming, features, conv_weight, head_weight, triple)

    triple = exchange(triple)
    values, triple = lax.optimization_barrier((values, triple))
    values = exchange(values)
    probs, value_grad = probs_of(triple, rows, pattern, live_blocks, order, share)

    value_grad, values = lax.optimization_barrier((value_grad, values))
    value_grad = exchange(value_grad)
    grads = grads_of(triple, rows, values, probs, pattern, live_blocks, order)
    grads, value_grad = lax.optimization_barrier((grads, value_grad))
    grads = exchange(grads)

    factor = 1.0 / math.sqrt(rows * devices)
    return tuple(unpack(grads, value_grad, conv_weight.shape, factor))


def solution(mesh):
    placed = (
        P(("clip", "ctx"), None),
        P(("clip", "ctx"), None),
        P(("clip", "ctx"), None),
        P(("clip", "ctx"), None, None),
        P(("clip", "ctx"), None, None),
        P(),
        P(),
        P("clip", None),
        P("clip"),
    )
    return jax.shard_map(
        body,
        mesh=mesh,
        in_specs=placed,
        out_specs=(
            P(("clip", "ctx"), None),
            P(("clip", "ctx"), None),
            P(("clip", "ctx"), None),
            P("clip", None, None),
        ),
        check_vma=False,
    )
```
